32 devices in a mesh: shock: 8 (over z, x), trans: 4 (over y, core).
Axes of the slice: x: 2, y: 2, z: 4, core: 2. Of those that a mesh axis runs over, the one named last changes fastest.
Arguments:
- conserved: float32 [11, 10, 65536], P(None, None, ('shock', 'trans')), may hold values from -6 to 6
- cell_size: float32 [65536], P(('shock', 'trans')), may hold values from 0.5 to 2
- sound_speed: float32 [65536], P(('shock', 'trans')), may hold values from 0.3 to 1.8
- jacobian: float32 [3, 11, 11], replicated, may hold values from -1.75 to 1.75
- derivative: float32 [3, 10, 10], replicated, may hold values from -2 to 2
- restriction: float32 [4, 6, 10], replicated, may hold values from -2 to 2
- lifting: float32 [4, 10, 6], replicated, may hold values from -2.5 to 2.5
- vertex_velocity: float32 [3, 16384], P(None, ('shock', 'trans')), may hold values from -1.8 to 1.8
- share_index: int32 [2, 4096], P(None, ('shock', 'trans')), may hold values from 0 to 511
- elem_vertex: int32 [4, 65536], P(None, ('shock', 'trans')), may hold values from 0 to 767
- inner_elem: int32 [2, 131072], P(None, ('shock', 'trans')), may hold values from 0 to 2047
- inner_face: int32 [2, 131072], P(None, ('shock', 'trans')), may hold values from 0 to 3
- inner_normal: float32 [3, 131072], P(None, ('shock', 'trans')), may hold values from -3 to 3
- slab_elem: int32 [2, 8192], P(None, ('shock', 'trans')), may hold values from 0 to 2047
- slab_face: int32 [2, 8192], P(None, ('shock', 'trans')), may hold values from 0 to 3
- slab_normal: float32 [3, 2, 8192], P(None, None, ('shock', 'trans')), may hold values from -3 to 3
- peer_elem: int32 [4, 2048], P(None, ('shock', 'trans')), may hold values from 0 to 2047
- peer_face: int32 [4, 2048], P(None, ('shock', 'trans')), may hold values from 0 to 3
- peer_normal: float32 [3, 4, 2048], P(None, None, ('shock', 'trans')), may hold values from -3 to 3
- peer_count: int32 [4, 32], P(None, ('shock', 'trans')), may hold values from 0 to 64, as said below
Outputs:
- rate: float32 [11, 10, 65536], P(None, None, ('shock', 'trans'))
- step_size: float32 [], replicated
The draws below stay inside these ranges and needn't reach their ends.
Inputs may be any that keep to these rules, and one draw needn't show every extreme that they name: peer_count[q, p] is the same for partition p at trans position q' and the partition of the same slab at position q when read from the other side, is 0 for q equal to p's own position, and equals 64 for some pair of each slab; slots at or past it are padding.
All inputs are finite; a program needn't handle non-finite values.
Results may differ from the reference program's by a relative error of at most 0.0003.
Values sent between devices are 32-bit elements; how exact they have to be, the bound alone decides.
A program may use at most 128 MiB of HBM per device.

```python
import math
import jax
import jax.numpy as jnp
from jax import lax

VARS = 11
BASIS = 10
FACE_BASIS = 6
EL_DEV = 2048
SLABS = 8
PEERS = 4
PARTITIONS = 32
ELEMS = 65536
SLAB_FACES = 256
PEER_FACES = 64
OWN_VERTS = 512
SHARED_VERTS = 128
INNER_FACES = 4096


def draw_sound_speed(key, part):
    position = jnp.arange(ELEMS, dtype=jnp.float32) / ELEMS
    spread = 0.3 * jnp.exp(jax.random.uniform(key, (ELEMS,), jnp.float32, 0.0, math.log(2.0)))
    return spread * jnp.exp(position * math.log(3.0))


def draw_peer_count(key, part):
    key_list = jax.random.split(key, 4)
    counts = jax.random.randint(key_list[0], (SLABS, PEERS, PEERS), PEER_FACES // 2, PEER_FACES + 1)
    living = jax.random.randint(key_list[1], (SLABS, PEERS, PEERS), 0, 5) < 4
    counts = jnp.where(living, counts, 0)
    grid_index = jnp.arange(PEERS)
    above_diag = grid_index[:, None] < grid_index[None, :]
    counts = jnp.where(above_diag[None], counts, jnp.swapaxes(counts, 1, 2))
    counts = jnp.where((grid_index[:, None] == grid_index[None, :])[None], 0, counts)
    first_peer = jax.random.randint(key_list[2], (SLABS,), 0, PEERS)
    second_peer = (first_peer + 1 + jax.random.randint(key_list[3], (SLABS,), 0, PEERS - 1)) % PEERS
    row_index = grid_index[None, :, None]
    col_index = grid_index[None, None, :]
    paired = (row_index == first_peer[:, None, None]) & (col_index == second_peer[:, None, None]) | (row_index == second_peer[:, None, None]) & (col_index == first_peer[:, None, None])
    counts = jnp.where(paired, PEER_FACES, counts)
    return jnp.transpose(counts, (2, 0, 1)).reshape(PEERS, SLABS * PEERS).astype(jnp.int32)


def place_ends(array, own_key, low, largest):
    longest = array.shape.index(max(array.shape))
    spots = []
    for shift in (0, 1):
        where = [jax.random.randint(jax.random.fold_in(own_key, axis), (), 0, length) for axis, length in enumerate(array.shape)]
        where[longest] = (where[longest] + shift) % array.shape[longest]
        spots.append(tuple(where))
    return array.at[spots[0]].set(low).at[spots[1]].set(largest)


def level_of(rng, extent, shards, low, largest):
    gain, own = 1.0, jax.random.fold_in(rng, 6)
    for dim, blocks in shards:
        draws = jnp.exp(jax.random.uniform(jax.random.fold_in(own, dim), (blocks,), jnp.float32, low / len(shards), largest / len(shards)))
        gain = gain * jnp.repeat(draws, extent[dim] // blocks).reshape([-1 if axis == dim else 1 for axis in range(len(extent))])
    return gain


def scatter_about(key, extent, deviation, limit, cuts=(), held_as=jnp.bfloat16):
    values = deviation * jax.random.normal(key, extent, jnp.float32)
    if cuts:
        values = values * level_of(key, extent, cuts, -0.22, 0.18)
    return jnp.clip(values, -limit, limit).astype(held_as)


def setup_inputs(seed: int = 0) -> dict:
    arg_keys = jax.random.split(jax.random.key(seed), 21)
    return {
        "conserved": scatter_about(arg_keys[0], (VARS, BASIS, ELEMS), 1.0, 6.0, ((2, 32),), jnp.float32),
        "cell_size": jnp.clip(jnp.exp(math.log(2.0) - 1.3862944 * jax.random.uniform(arg_keys[1], (ELEMS,), jnp.float32) ** level_of(arg_keys[1], (ELEMS,), ((0, 32),), -0.2, 0.2)), 0.5, 2.0),
        "sound_speed": draw_sound_speed(jax.random.fold_in(arg_keys[20], 71), 0),
        "jacobian": scatter_about(arg_keys[3], (3, VARS, VARS), VARS ** -0.5, 1.75, (), jnp.float32),
        "derivative": scatter_about(arg_keys[4], (3, BASIS, BASIS), BASIS ** -0.5, 2.0, (), jnp.float32),
        "restriction": scatter_about(arg_keys[5], (4, FACE_BASIS, BASIS), BASIS ** -0.5, 2.0, (), jnp.float32),
        "lifting": scatter_about(arg_keys[6], (4, BASIS, FACE_BASIS), FACE_BASIS ** -0.5, 2.5, (), jnp.float32),
        "vertex_velocity": scatter_about(arg_keys[7], (3, OWN_VERTS * PARTITIONS), 0.3, 1.8, ((1, 32),), jnp.float32),
        "share_index": place_ends(jax.random.randint(arg_keys[8], (2, SHARED_VERTS * PARTITIONS), 0, OWN_VERTS), jax.random.fold_in(arg_keys[8], 1), 0, OWN_VERTS - 1).astype(jnp.int32),
        "elem_vertex": place_ends(jax.random.randint(arg_keys[9], (4, ELEMS), 0, OWN_VERTS + 2 * SHARED_VERTS), jax.random.fold_in(arg_keys[9], 1), 0, (OWN_VERTS + 2 * SHARED_VERTS) - 1).astype(jnp.int32),
        "inner_elem": place_ends(jax.random.randint(arg_keys[10], (2, INNER_FACES * PARTITIONS), 0, EL_DEV), jax.random.fold_in(arg_keys[10], 1), 0, EL_DEV - 1).astype(jnp.int32),
        "inner_face": place_ends(jax.random.randint(arg_keys[11], (2, INNER_FACES * PARTITIONS), 0, 4), jax.random.fold_in(arg_keys[11], 1), 0, 3).astype(jnp.int32),
        "inner_normal": scatter_about(arg_keys[12], (3, INNER_FACES * PARTITIONS), 0.6, 3.0, ((1, 32),), jnp.float32),
        "slab_elem": place_ends(jax.random.randint(arg_keys[13], (2, SLAB_FACES * PARTITIONS), 0, EL_DEV), jax.random.fold_in(arg_keys[13], 1), 0, EL_DEV - 1).astype(jnp.int32),
        "slab_face": place_ends(jax.random.randint(arg_keys[14], (2, SLAB_FACES * PARTITIONS), 0, 4), jax.random.fold_in(arg_keys[14], 1), 0, 3).astype(jnp.int32),
        "slab_normal": scatter_about(arg_keys[15], (3, 2, SLAB_FACES * PARTITIONS), 0.6, 3.0, ((2, 32),), jnp.float32),
        "peer_elem": place_ends(jax.random.randint(arg_keys[16], (PEERS, PEER_FACES * PARTITIONS), 0, EL_DEV), jax.random.fold_in(arg_keys[16], 1), 0, EL_DEV - 1).astype(jnp.int32),
        "peer_face": place_ends(jax.random.randint(arg_keys[17], (PEERS, PEER_FACES * PARTITIONS), 0, 4), jax.random.fold_in(arg_keys[17], 1), 0, 3).astype(jnp.int32),
        "peer_normal": scatter_about(arg_keys[18], (3, PEERS, PEER_FACES * PARTITIONS), 0.6, 3.0, ((2, 32),), jnp.float32),
        "peer_count": draw_peer_count(jax.random.fold_in(arg_keys[20], 71), 0),
    }


HIGHEST_PREC = lax.Precision.HIGHEST
CFL_NUMBER = 0.3


def spatial(coeffs, mesh_vel, cell_scale, jacobian, derivative):
    summed = jnp.zeros_like(coeffs)
    for axis_dim in range(3):
        differentiated = jnp.einsum('vbe,cb->vce', coeffs, derivative[axis_dim], precision=HIGHEST_PREC)
        summed = summed + jnp.einsum('uv,vce->uce', jacobian[axis_dim], differentiated, precision=HIGHEST_PREC) - mesh_vel[axis_dim][None, None, :] * differentiated
    return summed / cell_scale[None, None, :]


def predict(coeffs, mesh_vel, cell_scale, step_size, jacobian, derivative):
    first_term = spatial(coeffs, mesh_vel, cell_scale, jacobian, derivative)
    second = spatial(first_term, mesh_vel, cell_scale, jacobian, derivative)
    return coeffs - (0.5 * step_size) * first_term + (step_size * step_size / 6.0) * second


def all_traces(predicted, restriction):
    num_vars = predicted.shape[0]
    elem_count = predicted.shape[2]
    face_table = jnp.einsum('kfb,vbe->vfke', restriction, predicted, precision=HIGHEST_PREC)
    return face_table.reshape(num_vars * restriction.shape[1], 4 * elem_count)


def pick(face_table, bound_row, elem_ids, face_ids, elem_count):
    return jnp.concatenate([face_table[:, face_ids * elem_count + elem_ids], bound_row[elem_ids][None, :]], axis=0)


def riemann(own_trace, theirs, normal, jacobian, face_basis):
    num_vars = jacobian.shape[1]
    face_count = own_trace.shape[1]
    inside = own_trace[:-1].reshape(num_vars, face_basis, face_count)
    outside = theirs[:-1].reshape(num_vars, face_basis, face_count)
    bound_max = jnp.maximum(own_trace[-1], theirs[-1])
    jump_value = outside - inside
    normal_flux = jnp.zeros_like(jump_value)
    for axis_dim in range(3):
        normal_flux = normal_flux + normal[axis_dim][None, None, :] * jnp.einsum('uv,vfn->ufn', jacobian[axis_dim], jump_value, precision=HIGHEST_PREC)
    return (0.5 * (normal_flux - bound_max[None, None, :] * jump_value)).reshape(num_vars * face_basis, face_count)


def face_rate(columns, values, lifting, num_vars, face_basis, elem_count):
    buffer = jnp.zeros((num_vars * face_basis, 4 * elem_count), jnp.float32).at[:, columns].add(values)
    return jnp.einsum('kbf,vfke->vbe', lifting, buffer.reshape(num_vars, face_basis, 4, elem_count), precision=HIGHEST_PREC)


def reference(conserved, cell_size, sound_speed, jacobian, derivative, restriction, lifting, vertex_velocity, share_index, elem_vertex, inner_elem, inner_face, inner_normal, slab_elem, slab_face, slab_normal, peer_elem, peer_face, peer_normal, peer_count):
    partitions = PARTITIONS
    elem_count = EL_DEV
    face_basis = FACE_BASIS
    num_vars = VARS
    states = jnp.moveaxis(conserved.reshape(VARS, BASIS, partitions, elem_count), 2, 0)
    scales = cell_size.reshape(partitions, elem_count)
    sounds = sound_speed.reshape(partitions, elem_count)
    velocity = jnp.moveaxis(vertex_velocity.reshape(3, partitions, OWN_VERTS), 1, 0)
    shares = jnp.moveaxis(share_index.reshape(2, partitions, SHARED_VERTS), 1, 0)
    down_set = jax.vmap(lambda vel_part, index_part: vel_part[:, index_part])(velocity, shares[:, 0])
    up_set = jax.vmap(lambda vel_part, index_part: vel_part[:, index_part])(velocity, shares[:, 1])
    up_grid = up_set.reshape(SLABS, PEERS, 3, SHARED_VERTS)
    down_grid = down_set.reshape(SLABS, PEERS, 3, SHARED_VERTS)
    from_lower = jnp.concatenate([jnp.zeros_like(up_grid[:1]), up_grid[:-1]], axis=0).reshape(partitions, 3, SHARED_VERTS)
    from_upper = jnp.concatenate([down_grid[1:], jnp.zeros_like(down_grid[:1])], axis=0).reshape(partitions, 3, SHARED_VERTS)
    vertex_table = jnp.concatenate([velocity, from_lower, from_upper], axis=2)
    corners = jnp.moveaxis(elem_vertex.reshape(4, partitions, elem_count), 1, 0)
    mesh_all = jax.vmap(lambda tab, cor: (tab[:, cor[0]] + tab[:, cor[1]] + tab[:, cor[2]] + tab[:, cor[3]]) * 0.25)(vertex_table, corners)
    wave_bound = sounds + jnp.abs(mesh_all[:, 0]) + jnp.abs(mesh_all[:, 1]) + jnp.abs(mesh_all[:, 2])
    step_size = CFL_NUMBER * jnp.min(scales / wave_bound)

    slab_e = jnp.moveaxis(slab_elem.reshape(2, partitions, SLAB_FACES), 1, 0).reshape(partitions, 2 * SLAB_FACES)
    slab_f = jnp.moveaxis(slab_face.reshape(2, partitions, SLAB_FACES), 1, 0).reshape(partitions, 2 * SLAB_FACES)
    slab_n = jnp.moveaxis(slab_normal.reshape(3, 2, partitions, SLAB_FACES), 2, 0).reshape(partitions, 3, 2 * SLAB_FACES)
    peer_e = jnp.moveaxis(peer_elem.reshape(PEERS, partitions, PEER_FACES), 1, 0).reshape(partitions, PEERS * PEER_FACES)
    peer_f = jnp.moveaxis(peer_face.reshape(PEERS, partitions, PEER_FACES), 1, 0).reshape(partitions, PEERS * PEER_FACES)
    peer_n = jnp.moveaxis(peer_normal.reshape(3, PEERS, partitions, PEER_FACES), 2, 0).reshape(partitions, 3, PEERS * PEER_FACES)
    peer_c = peer_count.reshape(PEERS, partitions).T
    inner_e = jnp.moveaxis(inner_elem.reshape(2, partitions, INNER_FACES), 1, 0)
    inner_f = jnp.moveaxis(inner_face.reshape(2, partitions, INNER_FACES), 1, 0)
    inner_n = jnp.moveaxis(inner_normal.reshape(3, partitions, INNER_FACES), 1, 0)

    def sends(packed):
        coeffs, cell_scale, mesh_vel, bound_row, s_elem, s_face, p_elem, p_face = packed
        predicted = predict(coeffs, mesh_vel, cell_scale, step_size, jacobian, derivative)
        face_table = all_traces(predicted, restriction)
        return (pick(face_table, bound_row, s_elem, s_face, elem_count), pick(face_table, bound_row, p_elem, p_face, elem_count))

    slab_send, peer_send = lax.map(sends, (states, scales, mesh_all, wave_bound, slab_e, slab_f, peer_e, peer_f))
    trace_rows = num_vars * face_basis + 1
    slab_grid = slab_send.reshape(SLABS, PEERS, trace_rows, 2 * SLAB_FACES)
    low_part = jnp.concatenate([jnp.zeros_like(slab_grid[:1, :, :, SLAB_FACES:]), slab_grid[:-1, :, :, SLAB_FACES:]], axis=0)
    high_part = jnp.concatenate([slab_grid[1:, :, :, :SLAB_FACES], jnp.zeros_like(slab_grid[:1, :, :, :SLAB_FACES])], axis=0)
    slab_recv = jnp.concatenate([low_part, high_part], axis=3).reshape(partitions, trace_rows, 2 * SLAB_FACES)
    peer_grid = peer_send.reshape(SLABS, PEERS, trace_rows, PEERS, PEER_FACES)
    peer_recv = jnp.transpose(peer_grid, (0, 3, 2, 1, 4)).reshape(partitions, trace_rows, PEERS * PEER_FACES)

    def rates(packed):
        (coeffs, cell_scale, mesh_vel, bound_row, s_elem, s_face, s_norm, s_recv,
         p_elem, p_face, p_norm, p_recv, p_cnt, i_elem, i_face, i_norm) = packed
        predicted = predict(coeffs, mesh_vel, cell_scale, step_size, jacobian, derivative)
        face_table = all_traces(predicted, restriction)
        slab_own = pick(face_table, bound_row, s_elem, s_face, elem_count)
        peer_own = pick(face_table, bound_row, p_elem, p_face, elem_count)
        side_zero = pick(face_table, bound_row, i_elem[0], i_face[0], elem_count)
        side_one = pick(face_table, bound_row, i_elem[1], i_face[1], elem_count)
        live_mask = (jnp.arange(PEER_FACES)[None, :] < p_cnt[:, None]).reshape(-1).astype(jnp.float32)
        values = jnp.concatenate([
            riemann(slab_own, s_recv, s_norm, jacobian, face_basis),
            riemann(peer_own, p_recv, p_norm, jacobian, face_basis) * live_mask[None, :],
            riemann(side_zero, side_one, i_norm, jacobian, face_basis),
            riemann(side_one, side_zero, -i_norm, jacobian, face_basis)], axis=1)
        columns = jnp.concatenate([s_face * elem_count + s_elem, p_face * elem_count + p_elem,
                                   i_face[0] * elem_count + i_elem[0], i_face[1] * elem_count + i_elem[1]])
        lifted = face_rate(columns, values, lifting, num_vars, face_basis, elem_count)
        return -(spatial(predicted, mesh_vel, cell_scale, jacobian, derivative) + lifted / cell_scale[None, None, :])

    result = lax.map(rates, (states, scales, mesh_all, wave_bound, slab_e, slab_f, slab_n, slab_recv,
                             peer_e, peer_f, peer_n, peer_recv, peer_c, inner_e, inner_f, inner_n))
    rate = jnp.moveaxis(result, 0, 2).reshape(VARS, BASIS, partitions * elem_count)
    return rate, step_size
```

```python
import functools

import jax
import jax.numpy as jnp
import numpy as np
from jax import lax
from jax.experimental import pallas as pl
from jax.experimental.pallas import tpu as pltpu
from jax.sharding import PartitionSpec as P

CFL_NUMBER = 0.3
F32 = jnp.float32
BF16 = jnp.bfloat16
MESH = pl.DeviceIdType.MESH
VMEM_BYTES = 56 * 1024 * 1024


def up_to(value, multiple):
    return -(-value // multiple) * multiple


def selections(num_vars, basis, face_basis, faces, rows, trace_rows):
    flat, flat_t = num_vars * basis, num_vars * face_basis
    row, trow = np.arange(rows), np.arange(trace_rows)
    row_v, row_b = np.where(row < flat, row // basis, -1), np.where(row < flat, row % basis, -1)
    trow_v = np.where(trow < flat_t, trow // face_basis, -2)
    trow_f = np.where(trow < flat_t, trow % face_basis, -2)

    def pick(target, count):
        return (target[:, None] == np.arange(count)[None, :]).astype(np.float32)

    def block(target, count, copies):
        out = np.zeros((copies, target.size, copies * count), np.float32)
        for k in range(copies):
            out[k, :, k * count : (k + 1) * count] = pick(target, count)
        return out.reshape(copies * target.size, copies * count)

    same_v = (row_v[:, None] == row_v[None, :]) & (row_v[:, None] >= 0)
    same_tv = (trow_v[:, None] == row_v[None, :]) & (trow_v[:, None] >= 0)
    same_f = (trow_f[:, None] == trow_f[None, :]) & (trow_f[:, None] >= 0)
    keep = np.zeros((trace_rows, rows), np.float32)
    keep[flat_t, flat] = 1.0
    return [
        np.ascontiguousarray(pick(row_v, num_vars).T),
        np.ascontiguousarray(pick(row_b, basis).T),
        block(row_v, num_vars, 3),
        block(row_b, basis, 3),
        block(trow_f, face_basis, faces),
        np.ascontiguousarray(pick(trow_v, num_vars).T),
        block(trow_v, num_vars, 3),
        pick(row_b, basis),
        np.ascontiguousarray(block(trow_f, face_basis, faces).T),
        same_v.astype(np.float32),
        same_tv.astype(np.float32),
        same_f.astype(np.float32),
        np.ascontiguousarray(same_tv.T.astype(np.float32)),
        keep,
    ]


def exact(a, b):
    return jnp.dot(a, b, precision=lax.Precision.HIGHEST, preferred_element_type=F32)


def dot(a, b):
    return jnp.dot(a, b, preferred_element_type=F32)


def split(value):
    high = value.astype(BF16)
    return high, (value - high.astype(F32)).astype(BF16)


def operator(matrix):
    high, low = split(matrix)
    return jnp.concatenate([high, high, low], axis=1)


def operand(value):
    high, low = split(value)
    return jnp.concatenate([high, low, high], axis=0)


def ones_at(index, count):
    places = lax.broadcasted_iota(jnp.int32, (count, index.shape[1]), 0)
    return jnp.where(places == index, 1.0, 0.0).astype(BF16)


def apply_space(space, value, mesh_vel, inverse, rows):
    product = dot(space, operand(value))
    total = product[:rows]
    for d in range(3):
        total = total - mesh_vel[d : d + 1] * product[(d + 1) * rows : (d + 2) * rows]
    return total * inverse


def gather_trace(table, ones, faces, trace_op, rows, trace_rows, num_faces):
    found = dot(table, ones)
    high, low = found[:rows].astype(BF16), found[rows:].astype(BF16)
    every = dot(trace_op, jnp.concatenate([high, low, high], axis=0))
    trace = jnp.where(faces == 0, every[:trace_rows], 0.0)
    for k in range(1, num_faces):
        trace = trace + jnp.where(faces == k, every[k * trace_rows : (k + 1) * trace_rows], 0.0)
    return trace


def front_kernel(
    sizes,
    conserved_ref,
    scalars_ref,
    vertex_ref,
    share_ref,
    corner_ref,
    jac_ref,
    der_ref,
    res_ref,
    lift_ref,
    bound_index_ref,
    sel_vt,
    sel_bt,
    sel_jac,
    sel_der,
    sel_res,
    sel_tvt,
    sel_tjac,
    sel_b,
    sel_lift,
    same_v,
    same_tv,
    same_f,
    same_vt,
    keep,
    table_ref,
    motion_ref,
    step_ref,
    own_ref,
    theirs_ref,
    space_ref,
    trace_ref,
    flux_ref,
    lifting_ref,
    state,
    first,
    second,
    ones,
    parts,
    vert_send,
    vert_recv,
    min_t,
    min_s,
    slab_send,
    slab_recv,
    peer_send,
    peer_recv,
    vert_sems,
    min_t_sems,
    min_s_sems,
    slab_sems,
    peer_sems,
):
    num_vars, basis, rows, trace_rows, num_faces, slabs, peers, chunk = sizes
    elems = conserved_ref.shape[2]
    shared = share_ref.shape[1]
    verts = vertex_ref.shape[1]
    slab_width = slab_send.shape[2]
    peer_width = peer_send.shape[2]
    send_rows = slab_send.shape[1]
    s = lax.axis_index("shock")
    t = lax.axis_index("trans")

    barrier = pltpu.get_barrier_semaphore()
    for o in range(1, peers):
        pl.semaphore_signal(
            barrier, inc=1, device_id=(s, lax.rem(t + o, peers)), device_id_type=MESH
        )
    for o in range(1, slabs):
        pl.semaphore_signal(
            barrier, inc=1, device_id=(lax.rem(s + o, slabs), t), device_id_type=MESH
        )

    def spread(velocity):
        high, low = split(velocity)
        rest = velocity - high.astype(F32) - low.astype(F32)
        return high.astype(F32), low.astype(F32), rest

    parts[...] = jnp.zeros_like(parts)
    for i, piece in enumerate(spread(vertex_ref[...])):
        parts[8 * i : 8 * i + 3, :verts] = piece
    share = jnp.concatenate([share_ref[0:1, :], share_ref[1:2, :]], axis=1)
    sent = dot(parts[:, :verts].astype(BF16), ones_at(share, verts))
    sent = sent[0:8] + sent[8:16] + sent[16:24]
    vert_send[0] = sent[:, :shared]
    vert_send[1] = sent[:, shared:]
    pl.semaphore_wait(barrier, peers - 1 + slabs - 1)

    def to_lower(source, dest, sems):
        return pltpu.make_async_remote_copy(
            src_ref=source.at[0],
            dst_ref=dest.at[1],
            send_sem=sems.at[0],
            recv_sem=sems.at[3],
            device_id=(s - 1, t),
            device_id_type=MESH,
        )

    def to_upper(source, dest, sems):
        return pltpu.make_async_remote_copy(
            src_ref=source.at[1],
            dst_ref=dest.at[0],
            send_sem=sems.at[1],
            recv_sem=sems.at[2],
            device_id=(s + 1, t),
            device_id_type=MESH,
        )

    def start_slab(source, dest, sems):
        @pl.when(s > 0)
        def _():
            to_lower(source, dest, sems).start()

        @pl.when(s < slabs - 1)
        def _():
            to_upper(source, dest, sems).start()

    def finish_slab(source, dest, sems):
        @pl.when(s > 0)
        def _():
            to_lower(source, dest, sems).wait_send()
            to_upper(source, dest, sems).wait_recv()

        @pl.when(s < slabs - 1)
        def _():
            to_upper(source, dest, sems).wait_send()
            to_lower(source, dest, sems).wait_recv()

        @pl.when(s == 0)
        def _():
            dest[0] = jnp.zeros(dest.shape[1:], F32)

        @pl.when(s == slabs - 1)
        def _():
            dest[1] = jnp.zeros(dest.shape[1:], F32)

    start_slab(vert_send, vert_recv, vert_sems)

    jac_wide = exact(sel_jac[...], exact(jac_ref[...], sel_vt[...]))
    der_wide = exact(sel_der[...], exact(der_ref[...], sel_bt[...]))
    both = jac_wide * der_wide
    space_ref[0:rows, :] = operator(both[:rows] + both[rows : 2 * rows] + both[2 * rows :])
    for d in range(3):
        space_ref[(d + 1) * rows : (d + 2) * rows, :] = operator(
            der_wide[d * rows : (d + 1) * rows] * same_v[...]
        )
    for v in range(num_vars):
        state[v * basis : (v + 1) * basis, :] = conserved_ref[v]
    state[num_vars * basis :, :] = jnp.zeros((rows - num_vars * basis, elems), F32)

    def counted(columns, low, count):
        places = lax.broadcasted_iota(jnp.int32, (count, chunk), 0) + low
        total = jnp.where(places == corner_ref[0:1, columns], 1.0, 0.0)
        for i in range(1, 4):
            total = total + jnp.where(places == corner_ref[i : i + 1, columns], 1.0, 0.0)
        return total.astype(BF16)

    own_parts = parts[:, :verts].astype(BF16)

    def own_corner(c, carry):
        columns = pl.ds(pl.multiple_of(c * chunk, chunk), chunk)
        found = dot(own_parts, counted(columns, 0, verts))
        motion_ref[:, columns] = found[0:8] + found[8:16] + found[16:24]
        return carry

    lax.fori_loop(0, elems // chunk, own_corner, 0)
    finish_slab(vert_send, vert_recv, vert_sems)
    for side in range(2):
        place = verts + side * shared
        for i, piece in enumerate(spread(vert_recv[side])):
            parts[8 * i : 8 * i + 8, place : place + shared] = piece
    far_parts = parts[:, verts:].astype(BF16)

    def far_corner(c, smallest):
        columns = pl.ds(pl.multiple_of(c * chunk, chunk), chunk)
        found = dot(far_parts, counted(columns, verts, 2 * shared))
        vel = 0.25 * (motion_ref[:, columns] + (found[0:8] + found[8:16] + found[16:24]))
        size = scalars_ref[0:1, columns]
        speed = (
            scalars_ref[1:2, columns] + jnp.abs(vel[0:1]) + jnp.abs(vel[1:2]) + jnp.abs(vel[2:3])
        )
        motion_ref[0:3, columns] = vel[0:3]
        motion_ref[3:4, columns] = 1.0 / size
        motion_ref[4:5, columns] = speed
        return jnp.minimum(smallest, jnp.min(size / speed, axis=1, keepdims=True))

    smallest = lax.fori_loop(0, elems // chunk, far_corner, jnp.full((1, 1), jnp.inf, F32))

    def min_copy(buffer, sems, place, count, o, along_trans):
        to = lax.rem(place + o, count)
        return pltpu.make_async_remote_copy(
            src_ref=buffer.at[place],
            dst_ref=buffer.at[place],
            send_sem=sems.at[0, o],
            recv_sem=sems.at[1, place],
            device_id=(s, to) if along_trans else (to, t),
            device_id_type=MESH,
        )

    def min_wait(buffer, sems, place, count, along_trans):
        for o in range(1, count):
            origin = lax.rem(place + count - o, count)
            pltpu.make_async_remote_copy(
                src_ref=buffer.at[origin],
                dst_ref=buffer.at[origin],
                send_sem=sems.at[0, o],
                recv_sem=sems.at[1, origin],
                device_id=(s, origin) if along_trans else (origin, t),
                device_id_type=MESH,
            ).wait_recv()
            min_copy(buffer, sems, place, count, o, along_trans).wait_send()

    min_t[t] = jnp.broadcast_to(smallest, min_t.shape[1:])
    for o in range(1, peers):
        min_copy(min_t, min_t_sems, t, peers, o, True).start()

    def space_step(source, dest):
        def one(c, carry):
            columns = pl.ds(pl.multiple_of(c * chunk, chunk), chunk)
            dest[:, columns] = apply_space(
                space_ref[...],
                source[:, columns],
                motion_ref[:, columns],
                motion_ref[3:4, columns],
                rows,
            )
            return carry

        lax.fori_loop(0, elems // chunk, one, 0)

    space_step(state, first)
    min_wait(min_t, min_t_sems, t, peers, True)
    best = min_t[0]
    for i in range(1, peers):
        best = jnp.minimum(best, min_t[i])
    min_s[s] = best
    for o in range(1, slabs):
        min_copy(min_s, min_s_sems, s, slabs, o, False).start()
    space_step(first, second)

    res_wide = exact(sel_res[...], exact(res_ref[...], sel_bt[...]))
    for k in range(num_faces):
        trace_ref[k * trace_rows : (k + 1) * trace_rows, :] = operator(
            res_wide[k * trace_rows : (k + 1) * trace_rows] * same_tv[...] + keep[...]
        )
    tjac_wide = exact(sel_tjac[...], exact(jac_ref[...], sel_tvt[...]))
    for d in range(3):
        flux_ref[d * trace_rows : (d + 1) * trace_rows, :] = operator(
            tjac_wide[d * trace_rows : (d + 1) * trace_rows] * same_f[...]
        )
    lift_wide = exact(sel_b[...], exact(lift_ref[...], sel_lift[...]))
    spread_v = jnp.concatenate([same_vt[...]] * num_faces, axis=1)
    lifting_ref[...] = operator(lift_wide * spread_v)
    ones[...] = ones_at(bound_index_ref[0:1, :], elems)

    min_wait(min_s, min_s_sems, s, slabs, False)
    best = min_s[0]
    for i in range(1, slabs):
        best = jnp.minimum(best, min_s[i])
    step = CFL_NUMBER * best
    step_ref[...] = step
    dt = step[0:1, 0:1]
    table_ref[...] = (
        state[...] - (0.5 * dt) * first[...] + (dt * dt * (1.0 / 6.0)) * second[...]
    )
    flat = num_vars * basis
    table_ref[flat : flat + 1, :] = motion_ref[4:5, :]
    high, low = split(table_ref[...])
    trace = gather_trace(
        jnp.concatenate([high, low], axis=0),
        ones[...],
        bound_index_ref[1:2, :],
        trace_ref[...],
        rows,
        trace_rows,
        num_faces,
    )
    own_ref[...] = trace
    cut = trace[:send_rows]
    slab_send[0] = cut[:, :slab_width]
    slab_send[1] = cut[:, slab_width : 2 * slab_width]
    for q in range(peers):
        low_end = 2 * slab_width + q * peer_width
        peer_send[q] = cut[:, low_end : low_end + peer_width]
    start_slab(slab_send, slab_recv, slab_sems)

    def peer_copy(o):
        to = lax.rem(t + o, peers)
        return pltpu.make_async_remote_copy(
            src_ref=peer_send.at[to],
            dst_ref=peer_recv.at[t],
            send_sem=peer_sems.at[0, o],
            recv_sem=peer_sems.at[1, t],
            device_id=(s, to),
            device_id_type=MESH,
        )

    for o in range(1, peers):
        peer_copy(o).start()
    peer_recv[t] = jnp.zeros(peer_recv.shape[1:], F32)
    theirs_ref[...] = jnp.zeros_like(theirs_ref)
    for o in range(1, peers):
        peer_copy(o).wait_send()
        origin = lax.rem(t + peers - o, peers)
        pltpu.make_async_remote_copy(
            src_ref=peer_send.at[origin],
            dst_ref=peer_recv.at[origin],
            send_sem=peer_sems.at[0, o],
            recv_sem=peer_sems.at[1, origin],
            device_id=(s, origin),
            device_id_type=MESH,
        ).wait_recv()
    for q in range(peers):
        low_end = 2 * slab_width + q * peer_width
        theirs_ref[:send_rows, low_end : low_end + peer_width] = peer_recv[q]
    finish_slab(slab_send, slab_recv, slab_sems)
    for side in range(2):
        theirs_ref[:send_rows, side * slab_width : (side + 1) * slab_width] = slab_recv[side]


def back_kernel(
    sizes,
    table_ref,
    motion_ref,
    own_ref,
    theirs_ref,
    space_ref,
    trace_ref,
    flux_ref,
    lifting_ref,
    bound_index_ref,
    bound_values_ref,
    inner_elem_ref,
    inner_face_ref,
    inner_normal_ref,
    rate_ref,
    table,
    ones,
    ones_bound,
    total,
):
    num_vars, basis, rows, trace_rows, num_faces, flat_trace, chunk, tile = sizes
    elems = table_ref.shape[1]
    high, low = split(table_ref[...])
    table[:rows, :] = high
    table[rows:, :] = low

    def normal_flux(jump, normal):
        product = dot(flux_ref[...], operand(jump))
        result = normal[0:1] * product[:trace_rows]
        for d in range(1, 3):
            result = result + normal[d : d + 1] * product[d * trace_rows : (d + 1) * trace_rows]
        return result

    def lifted(flux, faces, where_ones):
        high = flux.astype(BF16).astype(F32)
        low = flux - high
        highs = [jnp.where(faces == k, high, 0.0).astype(BF16) for k in range(num_faces)]
        lows = [jnp.where(faces == k, low, 0.0).astype(BF16) for k in range(num_faces)]
        value = dot(lifting_ref[...], jnp.concatenate(highs + lows + highs, axis=0))
        pair = jnp.concatenate(split(value), axis=0)
        return lax.dot_general(
            pair, where_ones, (((1,), (1,)), ((), ())), preferred_element_type=F32
        )

    faces = bound_index_ref[1:2, :]
    ones_bound[...] = ones_at(bound_index_ref[0:1, :], elems)
    own, theirs = own_ref[...], theirs_ref[...]
    jump = theirs - own
    bound = jnp.maximum(
        own[flat_trace : flat_trace + 1, :], theirs[flat_trace : flat_trace + 1, :]
    )
    flux = normal_flux(jump, bound_values_ref[...]) - bound * jump
    total[...] = lifted((0.5 * bound_values_ref[3:4, :]) * flux, faces, ones_bound[...])

    def inner(j, carry):
        columns = pl.ds(pl.multiple_of(j * tile, tile), tile)
        index = jnp.concatenate(
            [inner_elem_ref[0:1, columns], inner_elem_ref[1:2, columns]], axis=1
        )
        face = jnp.concatenate(
            [inner_face_ref[0:1, columns], inner_face_ref[1:2, columns]], axis=1
        )
        ones[...] = ones_at(index, elems)
        trace = gather_trace(
            table[...], ones[...], face, trace_ref[...], rows, trace_rows, num_faces
        )
        jump = trace[:, tile:] - trace[:, :tile]
        bound = jnp.maximum(
            trace[flat_trace : flat_trace + 1, :tile], trace[flat_trace : flat_trace + 1, tile:]
        )
        flow = normal_flux(jump, inner_normal_ref[:, columns])
        drop = bound * jump
        flux = 0.5 * jnp.concatenate([flow - drop, flow + drop], axis=1)
        total[...] += lifted(flux, face, ones[...])
        return carry

    lax.fori_loop(0, inner_elem_ref.shape[1] // tile, inner, 0)

    def finish(c, carry):
        columns = pl.ds(pl.multiple_of(c * chunk, chunk), chunk)
        inverse = motion_ref[3:4, columns]
        value = apply_space(
            space_ref[...], table_ref[:, columns], motion_ref[:, columns], inverse, rows
        )
        face_term = total[:rows, columns] + total[rows:, columns]
        rate = -(value + face_term * inverse)
        for v in range(num_vars):
            rate_ref[v, :, columns] = rate[v * basis : (v + 1) * basis]
        return carry

    lax.fori_loop(0, elems // chunk, finish, 0)


def body(
    conserved,
    cell_size,
    sound_speed,
    jacobian,
    derivative,
    restriction,
    lifting,
    vertex_velocity,
    share_index,
    elem_vertex,
    inner_elem,
    inner_face,
    inner_normal,
    slab_elem,
    slab_face,
    slab_normal,
    peer_elem,
    peer_face,
    peer_normal,
    peer_count,
):
    num_vars, basis, elems = conserved.shape
    num_faces, face_basis = restriction.shape[:2]
    slabs, peers = lax.axis_size("shock"), lax.axis_size("trans")
    slab_width, peer_width = slab_elem.shape[1], peer_elem.shape[1]
    verts, shared = vertex_velocity.shape[1], share_index.shape[1]
    rows = up_to(num_vars * basis + 1, 16)
    flat_trace = num_vars * face_basis
    trace_rows = up_to(flat_trace + 1, 16)
    send_rows = up_to(flat_trace + 1, 8)
    sides = 2 * slab_width + peers * peer_width
    chunk = min(512, elems)
    tile = min(512, inner_elem.shape[1])

    bound_index = jnp.stack(
        [
            jnp.concatenate([slab_elem.reshape(-1), peer_elem.reshape(-1)]),
            jnp.concatenate([slab_face.reshape(-1), peer_face.reshape(-1)]),
        ]
    )
    live = (jnp.arange(peer_width)[None, :] < peer_count).astype(F32).reshape(1, -1)
    bound_values = jnp.concatenate(
        [
            jnp.concatenate([slab_normal.reshape(3, -1), peer_normal.reshape(3, -1)], axis=1),
            jnp.concatenate([jnp.ones((1, 2 * slab_width), F32), live], axis=1),
        ],
        axis=0,
    )
    spreads = [
        jnp.asarray(a)
        for a in selections(num_vars, basis, face_basis, num_faces, rows, trace_rows)
    ]
    vmem = pl.BlockSpec(memory_space=pltpu.VMEM)
    out_shapes = (
        jax.ShapeDtypeStruct((rows, elems), F32),
        jax.ShapeDtypeStruct((8, elems), F32),
        jax.ShapeDtypeStruct((8, 128), F32),
        jax.ShapeDtypeStruct((trace_rows, sides), F32),
        jax.ShapeDtypeStruct((trace_rows, sides), F32),
        jax.ShapeDtypeStruct((4 * rows, 3 * rows), BF16),
        jax.ShapeDtypeStruct((num_faces * trace_rows, 3 * rows), BF16),
        jax.ShapeDtypeStruct((3 * trace_rows, 3 * trace_rows), BF16),
        jax.ShapeDtypeStruct((rows, 3 * num_faces * trace_rows), BF16),
    )
    front_args = [
        conserved,
        jnp.stack([cell_size, sound_speed]),
        vertex_velocity,
        share_index,
        elem_vertex,
        jacobian.reshape(3 * num_vars, num_vars),
        derivative.reshape(3 * basis, basis),
        restriction.reshape(num_faces * face_basis, basis),
        jnp.transpose(lifting, (1, 0, 2)).reshape(basis, num_faces * face_basis),
        bound_index,
        *spreads,
    ]
    dma = pltpu.SemaphoreType.DMA
    table, motion, step, own, theirs, space, trace, flux, lift = pl.pallas_call(
        functools.partial(
            front_kernel,
            (num_vars, basis, rows, trace_rows, num_faces, slabs, peers, chunk),
        ),
        out_shape=out_shapes,
        in_specs=[vmem] * len(front_args),
        out_specs=[vmem] * len(out_shapes),
        scratch_shapes=[
            pltpu.VMEM((rows, elems), F32),
            pltpu.VMEM((rows, elems), F32),
            pltpu.VMEM((rows, elems), F32),
            pltpu.VMEM((elems, sides), BF16),
            pltpu.VMEM((24, verts + 2 * shared), F32),
            pltpu.VMEM((2, 8, shared), F32),
            pltpu.VMEM((2, 8, shared), F32),
            pltpu.VMEM((peers, 8, 128), F32),
            pltpu.VMEM((slabs, 8, 128), F32),
            pltpu.VMEM((2, send_rows, slab_width), F32),
            pltpu.VMEM((2, send_rows, slab_width), F32),
            pltpu.VMEM((peers, send_rows, peer_width), F32),
            pltpu.VMEM((peers, send_rows, peer_width), F32),
            dma((4,)),
            dma((2, peers)),
            dma((2, slabs)),
            dma((4,)),
            dma((2, peers)),
        ],
        compiler_params=pltpu.CompilerParams(
            collective_id=0, has_side_effects=True, vmem_limit_bytes=VMEM_BYTES
        ),
        name="front",
    )(*front_args)

    back_args = [
        table,
        motion,
        own,
        theirs,
        space,
        trace,
        flux,
        lift,
        bound_index,
        bound_values,
        inner_elem,
        inner_face,
        inner_normal,
    ]
    rate = pl.pallas_call(
        functools.partial(
            back_kernel,
            (num_vars, basis, rows, trace_rows, num_faces, flat_trace, chunk, tile),
        ),
        out_shape=jax.ShapeDtypeStruct((num_vars, basis, elems), F32),
        in_specs=[vmem] * len(back_args),
        out_specs=vmem,
        scratch_shapes=[
            pltpu.VMEM((2 * rows, elems), BF16),
            pltpu.VMEM((elems, 2 * tile), BF16),
            pltpu.VMEM((elems, sides), BF16),
            pltpu.VMEM((2 * rows, elems), F32),
        ],
        compiler_params=pltpu.CompilerParams(vmem_limit_bytes=VMEM_BYTES),
        name="back",
    )(*back_args)
    return rate, step[0, 0]


def solution(mesh):
    both = ("shock", "trans")
    last2, last3 = P(None, both), P(None, None, both)
    return jax.shard_map(
        body,
        mesh=mesh,
        in_specs=(
            last3,
            P(both),
            P(both),
            P(),
            P(),
            P(),
            P(),
            last2,
            last2,
            last2,
            last2,
            last2,
            last2,
            last2,
            last2,
            last3,
            last2,
            last2,
            last3,
            last2,
        ),
        out_specs=(last3, P()),
        check_vma=False,
    )
```

```python
import functools

import jax
import jax.numpy as jnp
import numpy as np
from jax import lax
from jax.experimental import pallas as pl
from jax.experimental.pallas import tpu as pltpu
from jax.sharding import PartitionSpec as P

CFL_NUMBER = 0.3
F32 = jnp.float32
BF16 = jnp.bfloat16
MESH = pl.DeviceIdType.MESH
VMEM_BYTES = 56 * 1024 * 1024


def up_to(value, multiple):
    return -(-value // multiple) * multiple


def selections(num_vars, basis, face_basis, faces, rows, lift_rows, trace_rows):
    flat, flat_t = num_vars * basis, num_vars * face_basis
    row, trow = np.arange(rows), np.arange(trace_rows)
    row_v, row_b = (
        np.where(row < flat, row % num_vars, -1),
        np.where(row < flat, row // num_vars, -1),
    )
    lift_v, lift_b = (
        np.pad(a, (0, lift_rows - rows), constant_values=-1) for a in (row_v, row_b)
    )
    trow_v = np.where(trow < flat_t, trow // face_basis, -2)
    trow_f = np.where(trow < flat_t, trow % face_basis, -2)

    def pick(target, count):
        return (target[:, None] == np.arange(count)[None, :]).astype(np.float32)

    def block(target, count, copies):
        out = np.zeros((copies, target.size, copies * count), np.float32)
        for k in range(copies):
            out[k, :, k::copies] = pick(target, count)
        return out.reshape(copies * target.size, copies * count)

    same_v = (row_v[:, None] == row_v[None, :]) & (row_v[:, None] >= 0)
    same_vt = (lift_v[:, None] == trow_v[None, :]) & (lift_v[:, None] >= 0)
    same_tv = (trow_v[:, None] == row_v[None, :]) & (trow_v[:, None] >= 0)
    same_f = (trow_f[:, None] == trow_f[None, :]) & (trow_f[:, None] >= 0)
    keep = np.zeros((trace_rows, rows), np.float32)
    keep[flat_t, flat] = 1.0
    return [
        np.ascontiguousarray(pick(row_v, num_vars).T),
        np.ascontiguousarray(pick(row_b, basis).T),
        block(row_v, num_vars, 3),
        block(row_b, basis, 3),
        block(trow_f, face_basis, faces),
        np.ascontiguousarray(pick(trow_v, num_vars).T),
        block(trow_v, num_vars, 3),
        pick(lift_b, basis),
        np.ascontiguousarray(block(trow_f, face_basis, faces).T),
        same_v.astype(np.float32),
        same_tv.astype(np.float32),
        same_f.astype(np.float32),
        same_vt.astype(np.float32),
        keep,
    ]


def exact(a, b):
    return jnp.dot(a, b, precision=lax.Precision.HIGHEST, preferred_element_type=F32)


def dot(a, b):
    return jnp.dot(a, b, preferred_element_type=F32)


def split(value):
    high = value.astype(BF16)
    return high, (value - high.astype(F32)).astype(BF16)


def operator(matrix):
    high, low = split(matrix)
    return jnp.concatenate([high, high, low], axis=1)


def operand(value):
    high, low = split(value)
    return jnp.concatenate([high, low, high], axis=0)


def ones_at(index, count):
    places = lax.broadcasted_iota(jnp.int32, (count, index.shape[1]), 0)
    return jnp.where(places == index, 1.0, 0.0).astype(BF16)


def apply_space(space, value, mesh_vel, inverse, rows):
    product = dot(space, operand(value))
    total = product[:rows]
    for d in range(3):
        total = total - mesh_vel[d : d + 1] * product[(d + 1) * rows : (d + 2) * rows]
    return total * inverse


def gather_trace(table, ones, faces, trace_op, rows, trace_rows, num_faces):
    found = dot(table, ones)
    high, low = found[:rows].astype(BF16), found[rows:].astype(BF16)
    every = dot(trace_op, jnp.concatenate([high, low, high], axis=0))
    trace = jnp.where(faces == 0, every[:trace_rows], 0.0)
    for k in range(1, num_faces):
        trace = trace + jnp.where(faces == k, every[k * trace_rows : (k + 1) * trace_rows], 0.0)
    return trace


def front_kernel(
    sizes,
    conserved_ref,
    size_ref,
    sound_ref,
    vertex_ref,
    share_ref,
    corner_ref,
    jac_ref,
    der_ref,
    res_ref,
    lift_ref,
    slab_elem_ref,
    slab_face_ref,
    peer_elem_ref,
    peer_face_ref,
    slab_normal_ref,
    peer_normal_ref,
    count_ref,
    sel_vt,
    sel_bt,
    sel_jac,
    sel_der,
    sel_res,
    sel_tvt,
    sel_tjac,
    sel_b,
    sel_lift,
    same_v,
    same_tv,
    same_f,
    same_vt,
    keep,
    table_ref,
    motion_ref,
    step_ref,
    own_ref,
    theirs_ref,
    space_ref,
    trace_ref,
    flux_ref,
    lifting_ref,
    bound_index_ref,
    bound_values_ref,
    state,
    first,
    second,
    ones,
    parts,
    jac,
    der,
    res,
    lift,
    vert_send,
    vert_recv,
    min_t,
    min_s,
    slab_send,
    slab_recv,
    peer_send,
    peer_recv,
    vert_sems,
    min_t_sems,
    min_s_sems,
    slab_sems,
    peer_sems,
):
    num_vars, basis, rows, trace_rows, num_faces, slabs, peers, chunk = sizes
    elems = conserved_ref.shape[2]
    shared = share_ref.shape[1]
    verts = vertex_ref.shape[1]
    slab_width = slab_send.shape[2]
    peer_width = peer_send.shape[2]
    send_rows = slab_send.shape[1]
    s = lax.axis_index("shock")
    t = lax.axis_index("trans")

    barrier = pltpu.get_barrier_semaphore()
    for o in range(1, peers):
        pl.semaphore_signal(
            barrier, inc=1, device_id=(s, lax.rem(t + o, peers)), device_id_type=MESH
        )
    for o in range(1, slabs):
        pl.semaphore_signal(
            barrier, inc=1, device_id=(lax.rem(s + o, slabs), t), device_id_type=MESH
        )

    def spread(velocity):
        high, low = split(velocity)
        rest = velocity - high.astype(F32) - low.astype(F32)
        return high.astype(F32), low.astype(F32), rest

    parts[...] = jnp.zeros_like(parts)
    for i, piece in enumerate(spread(vertex_ref[...])):
        parts[8 * i : 8 * i + 3, :verts] = piece
    share = jnp.concatenate([share_ref[0:1, :], share_ref[1:2, :]], axis=1)
    sent = dot(parts[:, :verts].astype(BF16), ones_at(share, verts))
    sent = sent[0:8] + sent[8:16] + sent[16:24]
    vert_send[0] = sent[:, :shared]
    vert_send[1] = sent[:, shared:]
    pl.semaphore_wait(barrier, peers - 1 + slabs - 1)

    def to_lower(source, dest, sems):
        return pltpu.make_async_remote_copy(
            src_ref=source.at[0],
            dst_ref=dest.at[1],
            send_sem=sems.at[0],
            recv_sem=sems.at[3],
            device_id=(s - 1, t),
            device_id_type=MESH,
        )

    def to_upper(source, dest, sems):
        return pltpu.make_async_remote_copy(
            src_ref=source.at[1],
            dst_ref=dest.at[0],
            send_sem=sems.at[1],
            recv_sem=sems.at[2],
            device_id=(s + 1, t),
            device_id_type=MESH,
        )

    def start_slab(source, dest, sems):
        @pl.when(s > 0)
        def _():
            to_lower(source, dest, sems).start()

        @pl.when(s < slabs - 1)
        def _():
            to_upper(source, dest, sems).start()

    def finish_slab(source, dest, sems):
        @pl.when(s > 0)
        def _():
            to_lower(source, dest, sems).wait_send()
            to_upper(source, dest, sems).wait_recv()

        @pl.when(s < slabs - 1)
        def _():
            to_upper(source, dest, sems).wait_send()
            to_lower(source, dest, sems).wait_recv()

        @pl.when(s == 0)
        def _():
            dest[0] = jnp.zeros(dest.shape[1:], F32)

        @pl.when(s == slabs - 1)
        def _():
            dest[1] = jnp.zeros(dest.shape[1:], F32)

    start_slab(vert_send, vert_recv, vert_sems)

    for small, held in ((jac_ref, jac), (der_ref, der), (res_ref, res), (lift_ref, lift)):
        count = small.shape[1]
        for i in range(small.shape[0]):
            held[i * count : (i + 1) * count, :] = small[i]
    jac_wide = exact(sel_jac[...], exact(jac[...], sel_vt[...]))
    der_wide = exact(sel_der[...], exact(der[...], sel_bt[...]))
    both = jac_wide * der_wide
    space_ref[0:rows, :] = operator(both[:rows] + both[rows : 2 * rows] + both[2 * rows :])
    for d in range(3):
        space_ref[(d + 1) * rows : (d + 2) * rows, :] = operator(
            der_wide[d * rows : (d + 1) * rows] * same_v[...]
        )
    for b in range(basis):
        state[b * num_vars : (b + 1) * num_vars, :] = conserved_ref[b]
    state[num_vars * basis :, :] = jnp.zeros((rows - num_vars * basis, elems), F32)

    def counted(columns, low, count):
        places = lax.broadcasted_iota(jnp.int32, (count, chunk), 0) + low
        total = jnp.where(places == corner_ref[0:1, columns], 1.0, 0.0)
        for i in range(1, 4):
            total = total + jnp.where(places == corner_ref[i : i + 1, columns], 1.0, 0.0)
        return total.astype(BF16)

    own_parts = parts[:, :verts].astype(BF16)

    def own_corner(c, carry):
        columns = pl.ds(pl.multiple_of(c * chunk, chunk), chunk)
        found = dot(own_parts, counted(columns, 0, verts))
        motion_ref[:, columns] = found[0:8] + found[8:16] + found[16:24]
        return carry

    lax.fori_loop(0, elems // chunk, own_corner, 0)
    finish_slab(vert_send, vert_recv, vert_sems)
    for side in range(2):
        place = verts + side * shared
        for i, piece in enumerate(spread(vert_recv[side])):
            parts[8 * i : 8 * i + 8, place : place + shared] = piece
    far_parts = parts[:, verts:].astype(BF16)

    def far_corner(c, smallest):
        columns = pl.ds(pl.multiple_of(c * chunk, chunk), chunk)
        found = dot(far_parts, counted(columns, verts, 2 * shared))
        vel = 0.25 * (motion_ref[:, columns] + (found[0:8] + found[8:16] + found[16:24]))
        size = size_ref[0:1, columns]
        speed = (
            sound_ref[0:1, columns] + jnp.abs(vel[0:1]) + jnp.abs(vel[1:2]) + jnp.abs(vel[2:3])
        )
        motion_ref[0:3, columns] = vel[0:3]
        motion_ref[3:4, columns] = 1.0 / size
        motion_ref[4:5, columns] = speed
        return jnp.minimum(smallest, jnp.min(size / speed, axis=1, keepdims=True))

    smallest = lax.fori_loop(0, elems // chunk, far_corner, jnp.full((1, 1), jnp.inf, F32))

    def min_copy(buffer, sems, place, count, o, along_trans):
        to = lax.rem(place + o, count)
        return pltpu.make_async_remote_copy(
            src_ref=buffer.at[place],
            dst_ref=buffer.at[place],
            send_sem=sems.at[0, o],
            recv_sem=sems.at[1, place],
            device_id=(s, to) if along_trans else (to, t),
            device_id_type=MESH,
        )

    def min_wait(buffer, sems, place, count, along_trans):
        for o in range(1, count):
            origin = lax.rem(place + count - o, count)
            pltpu.make_async_remote_copy(
                src_ref=buffer.at[origin],
                dst_ref=buffer.at[origin],
                send_sem=sems.at[0, o],
                recv_sem=sems.at[1, origin],
                device_id=(s, origin) if along_trans else (origin, t),
                device_id_type=MESH,
            ).wait_recv()
            min_copy(buffer, sems, place, count, o, along_trans).wait_send()

    min_t[t] = jnp.broadcast_to(smallest, min_t.shape[1:])
    for o in range(1, peers):
        min_copy(min_t, min_t_sems, t, peers, o, True).start()

    def space_step(source, dest):
        def one(c, carry):
            columns = pl.ds(pl.multiple_of(c * chunk, chunk), chunk)
            dest[:, columns] = apply_space(
                space_ref[...],
                source[:, columns],
                motion_ref[:, columns],
                motion_ref[3:4, columns],
                rows,
            )
            return carry

        lax.fori_loop(0, elems // chunk, one, 0)

    space_step(state, first)
    min_wait(min_t, min_t_sems, t, peers, True)
    best = min_t[0]
    for i in range(1, peers):
        best = jnp.minimum(best, min_t[i])
    min_s[s] = best
    for o in range(1, slabs):
        min_copy(min_s, min_s_sems, s, slabs, o, False).start()
    space_step(first, second)

    res_wide = exact(sel_res[...], exact(res[...], sel_bt[...]))
    for k in range(num_faces):
        trace_ref[k * trace_rows : (k + 1) * trace_rows, :] = operator(
            res_wide[k * trace_rows : (k + 1) * trace_rows] * same_tv[...] + keep[...]
        )
    tjac_wide = exact(sel_tjac[...], exact(jac[...], sel_tvt[...]))
    for d in range(3):
        flux_ref[d * trace_rows : (d + 1) * trace_rows, :] = operator(
            tjac_wide[d * trace_rows : (d + 1) * trace_rows] * same_f[...]
        )
    lift_rows = lax.dot_general(
        sel_b[...],
        lift[...],
        (((1,), (1,)), ((), ())),
        precision=lax.Precision.HIGHEST,
        preferred_element_type=F32,
    )
    lift_wide = exact(lift_rows, sel_lift[...])
    spread_v = jnp.concatenate([same_vt[...]] * num_faces, axis=1)
    lifting_ref[...] = operator(lift_wide * spread_v)
    for row, slab_ref, peer_ref in (
        (0, slab_elem_ref, peer_elem_ref),
        (1, slab_face_ref, peer_face_ref),
    ):
        for side in range(2):
            bound_index_ref[row : row + 1, side * slab_width : (side + 1) * slab_width] = slab_ref[
                side : side + 1, :
            ]
        for q in range(peers):
            low_end = 2 * slab_width + q * peer_width
            bound_index_ref[row : row + 1, low_end : low_end + peer_width] = peer_ref[
                q : q + 1, :
            ]
    for d in range(3):
        for side in range(2):
            bound_values_ref[d : d + 1, side * slab_width : (side + 1) * slab_width] = (
                slab_normal_ref[d, side : side + 1, :]
            )
        for q in range(peers):
            low_end = 2 * slab_width + q * peer_width
            bound_values_ref[d : d + 1, low_end : low_end + peer_width] = peer_normal_ref[
                d, q : q + 1, :
            ]
    bound_values_ref[3:4, : 2 * slab_width] = jnp.ones((1, 2 * slab_width), F32)
    slot = lax.broadcasted_iota(jnp.int32, (1, peer_width), 1)
    for q in range(peers):
        low_end = 2 * slab_width + q * peer_width
        bound_values_ref[3:4, low_end : low_end + peer_width] = jnp.where(
            slot < count_ref[0:1, q : q + 1], 1.0, 0.0
        )
    ones[...] = ones_at(bound_index_ref[0:1, :], elems)

    min_wait(min_s, min_s_sems, s, slabs, False)
    best = min_s[0]
    for i in range(1, slabs):
        best = jnp.minimum(best, min_s[i])
    step = CFL_NUMBER * best
    step_ref[...] = step
    dt = step[0:1, 0:1]
    table_ref[...] = (
        state[...] - (0.5 * dt) * first[...] + (dt * dt * (1.0 / 6.0)) * second[...]
    )
    flat = num_vars * basis
    table_ref[flat : flat + 1, :] = motion_ref[4:5, :]
    high, low = split(table_ref[...])
    trace = gather_trace(
        jnp.concatenate([high, low], axis=0),
        ones[...],
        bound_index_ref[1:2, :],
        trace_ref[...],
        rows,
        trace_rows,
        num_faces,
    )
    own_ref[...] = trace
    cut = trace[:send_rows]
    slab_send[0] = cut[:, :slab_width]
    slab_send[1] = cut[:, slab_width : 2 * slab_width]
    for q in range(peers):
        low_end = 2 * slab_width + q * peer_width
        peer_send[q] = cut[:, low_end : low_end + peer_width]
    start_slab(slab_send, slab_recv, slab_sems)

    def peer_copy(o):
        to = lax.rem(t + o, peers)
        return pltpu.make_async_remote_copy(
            src_ref=peer_send.at[to],
            dst_ref=peer_recv.at[t],
            send_sem=peer_sems.at[0, o],
            recv_sem=peer_sems.at[1, t],
            device_id=(s, to),
            device_id_type=MESH,
        )

    for o in range(1, peers):
        peer_copy(o).start()
    peer_recv[t] = jnp.zeros(peer_recv.shape[1:], F32)
    theirs_ref[...] = jnp.zeros_like(theirs_ref)
    for o in range(1, peers):
        peer_copy(o).wait_send()
        origin = lax.rem(t + peers - o, peers)
        pltpu.make_async_remote_copy(
            src_ref=peer_send.at[origin],
            dst_ref=peer_recv.at[origin],
            send_sem=peer_sems.at[0, o],
            recv_sem=peer_sems.at[1, origin],
            device_id=(s, origin),
            device_id_type=MESH,
        ).wait_recv()
    for q in range(peers):
        low_end = 2 * slab_width + q * peer_width
        theirs_ref[:send_rows, low_end : low_end + peer_width] = peer_recv[q]
    finish_slab(slab_send, slab_recv, slab_sems)
    for side in range(2):
        theirs_ref[:send_rows, side * slab_width : (side + 1) * slab_width] = slab_recv[side]


def back_kernel(
    sizes,
    table_ref,
    motion_ref,
    own_ref,
    theirs_ref,
    space_ref,
    trace_ref,
    flux_ref,
    lifting_ref,
    bound_index_ref,
    bound_values_ref,
    inner_elem_ref,
    inner_face_ref,
    inner_normal_ref,
    step_ref,
    rate_ref,
    step_out_ref,
    table,
    ones,
    ones_bound,
    total,
):
    num_vars, basis, rows, trace_rows, num_faces, flat_trace, chunk, tile = sizes
    elems = table_ref.shape[1]
    lift_rows = lifting_ref.shape[0]
    step_out_ref[0, 0] = step_ref[0, 0]
    high, low = split(table_ref[...])
    table[:rows, :] = high
    table[rows:, :] = low

    def normal_flux(jump, normal):
        product = dot(flux_ref[...], operand(jump))
        result = normal[0:1] * product[:trace_rows]
        for d in range(1, 3):
            result = result + normal[d : d + 1] * product[d * trace_rows : (d + 1) * trace_rows]
        return result

    def lifted(flux, faces, where_ones):
        high = flux.astype(BF16).astype(F32)
        low = flux - high
        highs = [jnp.where(faces == k, high, 0.0).astype(BF16) for k in range(num_faces)]
        lows = [jnp.where(faces == k, low, 0.0).astype(BF16) for k in range(num_faces)]
        value = dot(lifting_ref[...], jnp.concatenate(highs + lows + highs, axis=0))
        pair = jnp.concatenate(split(value), axis=0)
        return lax.dot_general(
            where_ones, pair, (((1,), (1,)), ((), ())), preferred_element_type=F32
        )

    faces = bound_index_ref[1:2, :]
    ones_bound[...] = ones_at(bound_index_ref[0:1, :], elems)
    own, theirs = own_ref[...], theirs_ref[...]
    jump = theirs - own
    bound = jnp.maximum(
        own[flat_trace : flat_trace + 1, :], theirs[flat_trace : flat_trace + 1, :]
    )
    flux = normal_flux(jump, bound_values_ref[...]) - bound * jump
    total[...] = lifted((0.5 * bound_values_ref[3:4, :]) * flux, faces, ones_bound[...])

    def inner(j, carry):
        columns = pl.ds(pl.multiple_of(j * tile, tile), tile)
        index = jnp.concatenate(
            [inner_elem_ref[0:1, columns], inner_elem_ref[1:2, columns]], axis=1
        )
        face = jnp.concatenate(
            [inner_face_ref[0:1, columns], inner_face_ref[1:2, columns]], axis=1
        )
        ones[...] = ones_at(index, elems)
        trace = gather_trace(
            table[...], ones[...], face, trace_ref[...], rows, trace_rows, num_faces
        )
        jump = trace[:, tile:] - trace[:, :tile]
        bound = jnp.maximum(
            trace[flat_trace : flat_trace + 1, :tile], trace[flat_trace : flat_trace + 1, tile:]
        )
        flow = normal_flux(jump, inner_normal_ref[:, columns])
        drop = bound * jump
        flux = 0.5 * jnp.concatenate([flow - drop, flow + drop], axis=1)
        total[...] += lifted(flux, face, ones[...])
        return carry

    lax.fori_loop(0, inner_elem_ref.shape[1] // tile, inner, 0)

    def finish(c, carry):
        columns = pl.ds(pl.multiple_of(c * chunk, chunk), chunk)
        inverse = motion_ref[3:4, columns]
        value = apply_space(
            space_ref[...], table_ref[:, columns], motion_ref[:, columns], inverse, rows
        )
        face_term = jnp.transpose(total[columns, :lift_rows] + total[columns, lift_rows:])
        rate = -(value + face_term[:rows] * inverse)
        for b in range(basis):
            rate_ref[b, :, columns] = rate[b * num_vars : (b + 1) * num_vars]
        return carry

    lax.fori_loop(0, elems // chunk, finish, 0)


def body(
    conserved,
    cell_size,
    sound_speed,
    jacobian,
    derivative,
    restriction,
    lifting,
    vertex_velocity,
    share_index,
    elem_vertex,
    inner_elem,
    inner_face,
    inner_normal,
    slab_elem,
    slab_face,
    slab_normal,
    peer_elem,
    peer_face,
    peer_normal,
    peer_count,
):
    num_vars, basis, elems = conserved.shape
    num_faces, face_basis = restriction.shape[:2]
    slabs, peers = lax.axis_size("shock"), lax.axis_size("trans")
    slab_width, peer_width = slab_elem.shape[1], peer_elem.shape[1]
    verts, shared = vertex_velocity.shape[1], share_index.shape[1]
    rows = up_to(num_vars * basis + 1, 16)
    lift_rows = up_to(rows, 128)
    flat_trace = num_vars * face_basis
    trace_rows = up_to(flat_trace + 1, 16)
    send_rows = up_to(flat_trace + 1, 8)
    sides = 2 * slab_width + peers * peer_width
    chunk = min(512, elems)
    tile = min(512, inner_elem.shape[1])

    spreads = [
        jnp.asarray(a)
        for a in selections(num_vars, basis, face_basis, num_faces, rows, lift_rows, trace_rows)
    ]
    vmem = pl.BlockSpec(memory_space=pltpu.VMEM)
    out_shapes = (
        jax.ShapeDtypeStruct((rows, elems), F32),
        jax.ShapeDtypeStruct((8, elems), F32),
        jax.ShapeDtypeStruct((8, 128), F32),
        jax.ShapeDtypeStruct((trace_rows, sides), F32),
        jax.ShapeDtypeStruct((trace_rows, sides), F32),
        jax.ShapeDtypeStruct((4 * rows, 3 * rows), BF16),
        jax.ShapeDtypeStruct((num_faces * trace_rows, 3 * rows), BF16),
        jax.ShapeDtypeStruct((3 * trace_rows, 3 * trace_rows), BF16),
        jax.ShapeDtypeStruct((lift_rows, 3 * num_faces * trace_rows), BF16),
        jax.ShapeDtypeStruct((2, sides), jnp.int32),
        jax.ShapeDtypeStruct((4, sides), F32),
    )
    front_args = [
        jnp.transpose(conserved, (1, 0, 2)),
        cell_size.reshape(1, elems),
        sound_speed.reshape(1, elems),
        vertex_velocity,
        share_index,
        elem_vertex,
        jnp.transpose(jacobian, (1, 0, 2)),
        jnp.transpose(derivative, (1, 0, 2)),
        jnp.transpose(restriction, (1, 0, 2)),
        jnp.transpose(lifting, (2, 0, 1)),
        slab_elem,
        slab_face,
        peer_elem,
        peer_face,
        slab_normal,
        peer_normal,
        jnp.transpose(peer_count),
        *spreads,
    ]
    dma = pltpu.SemaphoreType.DMA
    table, motion, step, own, theirs, space, trace, flux, lift, bound_index, bound_values = pl.pallas_call(
        functools.partial(
            front_kernel,
            (num_vars, basis, rows, trace_rows, num_faces, slabs, peers, chunk),
        ),
        out_shape=out_shapes,
        in_specs=[vmem] * len(front_args),
        out_specs=[vmem] * len(out_shapes),
        scratch_shapes=[
            pltpu.VMEM((rows, elems), F32),
            pltpu.VMEM((rows, elems), F32),
            pltpu.VMEM((rows, elems), F32),
            pltpu.VMEM((elems, sides), BF16),
            pltpu.VMEM((24, verts + 2 * shared), F32),
            pltpu.VMEM((3 * num_vars, num_vars), F32),
            pltpu.VMEM((3 * basis, basis), F32),
            pltpu.VMEM((num_faces * face_basis, basis), F32),
            pltpu.VMEM((num_faces * face_basis, basis), F32),
            pltpu.VMEM((2, 8, shared), F32),
            pltpu.VMEM((2, 8, shared), F32),
            pltpu.VMEM((peers, 8, 128), F32),
            pltpu.VMEM((slabs, 8, 128), F32),
            pltpu.VMEM((2, send_rows, slab_width), F32),
            pltpu.VMEM((2, send_rows, slab_width), F32),
            pltpu.VMEM((peers, send_rows, peer_width), F32),
            pltpu.VMEM((peers, send_rows, peer_width), F32),
            dma((4,)),
            dma((2, peers)),
            dma((2, slabs)),
            dma((4,)),
            dma((2, peers)),
        ],
        compiler_params=pltpu.CompilerParams(
            collective_id=0, has_side_effects=True, vmem_limit_bytes=VMEM_BYTES
        ),
        name="front",
    )(*front_args)

    back_args = [
        table,
        motion,
        own,
        theirs,
        space,
        trace,
        flux,
        lift,
        bound_index,
        bound_values,
        inner_elem,
        inner_face,
        inner_normal,
        step,
    ]
    rate, step = pl.pallas_call(
        functools.partial(
            back_kernel,
            (num_vars, basis, rows, trace_rows, num_faces, flat_trace, chunk, tile),
        ),
        out_shape=(
            jax.ShapeDtypeStruct((basis, num_vars, elems), F32),
            jax.ShapeDtypeStruct((1, 1), F32),
        ),
        in_specs=[vmem] * (len(back_args) - 1) + [pl.BlockSpec(memory_space=pltpu.SMEM)],
        out_specs=(vmem, pl.BlockSpec(memory_space=pltpu.SMEM)),
        scratch_shapes=[
            pltpu.VMEM((2 * rows, elems), BF16),
            pltpu.VMEM((elems, 2 * tile), BF16),
            pltpu.VMEM((elems, sides), BF16),
            pltpu.VMEM((elems, 2 * lift_rows), F32),
        ],
        compiler_params=pltpu.CompilerParams(vmem_limit_bytes=VMEM_BYTES),
        name="back",
    )(*back_args)
    return jnp.transpose(rate, (1, 0, 2)), step.reshape(())


def solution(mesh):
    both = ("shock", "trans")
    last2, last3 = P(None, both), P(None, None, both)
    return jax.shard_map(
        body,
        mesh=mesh,
        in_specs=(
            last3,
            P(both),
            P(both),
            P(),
            P(),
            P(),
            P(),
            last2,
            last2,
            last2,
            last2,
            last2,
            last2,
            last2,
            last2,
            last3,
            last2,
            last2,
            last3,
            last2,
        ),
        out_specs=(last3, P()),
        check_vma=False,
    )
```

```python
import functools

import jax
import jax.numpy as jnp
import numpy as np
from jax import lax
from jax.experimental import pallas as pl
from jax.experimental.pallas import tpu as pltpu
from jax.sharding import PartitionSpec as P

CFL_NUMBER = 0.3
F32 = jnp.float32
BF16 = jnp.bfloat16
MESH = pl.DeviceIdType.MESH
VMEM_BYTES = 56 * 1024 * 1024


def up_to(value, multiple):
    return -(-value // multiple) * multiple


def selections(num_vars, basis, face_basis, faces, rows, lift_rows, trace_rows):
    flat, flat_t = num_vars * basis, num_vars * face_basis
    row, trow = np.arange(rows), np.arange(trace_rows)
    row_v, row_b = (
        np.where(row < flat, row % num_vars, -1),
        np.where(row < flat, row // num_vars, -1),
    )
    lift_v, lift_b = (
        np.pad(a, (0, lift_rows - rows), constant_values=-1) for a in (row_v, row_b)
    )
    trow_v = np.where(trow < flat_t, trow // face_basis, -2)
    trow_f = np.where(trow < flat_t, trow % face_basis, -2)

    def pick(target, count):
        return (target[:, None] == np.arange(count)[None, :]).astype(np.float32)

    def block(target, count, copies):
        out = np.zeros((copies, target.size, copies * count), np.float32)
        for k in range(copies):
            out[k, :, k::copies] = pick(target, count)
        return out.reshape(copies * target.size, copies * count)

    same_v = (row_v[:, None] == row_v[None, :]) & (row_v[:, None] >= 0)
    same_vt = (lift_v[:, None] == trow_v[None, :]) & (lift_v[:, None] >= 0)
    same_tv = (trow_v[:, None] == row_v[None, :]) & (trow_v[:, None] >= 0)
    same_f = (trow_f[:, None] == trow_f[None, :]) & (trow_f[:, None] >= 0)
    keep = np.zeros((trace_rows, rows), np.float32)
    keep[flat_t, flat] = 1.0
    return [
        np.ascontiguousarray(pick(row_v, num_vars).T),
        np.ascontiguousarray(pick(row_b, basis).T),
        block(row_v, num_vars, 3),
        block(row_b, basis, 3),
        block(trow_f, face_basis, faces),
        np.ascontiguousarray(pick(trow_v, num_vars).T),
        block(trow_v, num_vars, 3),
        pick(lift_b, basis),
        np.ascontiguousarray(block(trow_f, face_basis, faces).T),
        same_v.astype(np.float32),
        same_tv.astype(np.float32),
        same_f.astype(np.float32),
        same_vt.astype(np.float32),
        keep,
    ]


def exact(a, b):
    return jnp.dot(a, b, precision=lax.Precision.HIGHEST, preferred_element_type=F32)


def dot(a, b):
    return jnp.dot(a, b, preferred_element_type=F32)


def split(value):
    high = value.astype(BF16)
    return high, (value - high.astype(F32)).astype(BF16)


def operator(matrix):
    high, low = split(matrix)
    return jnp.concatenate([high, high, low], axis=1)


def operand(value):
    high, low = split(value)
    return jnp.concatenate([high, low, high], axis=0)


def ones_at(index, count):
    places = lax.broadcasted_iota(jnp.int32, (count, index.shape[1]), 0)
    return jnp.where(places == index, 1.0, 0.0).astype(BF16)


def apply_space(space, value, mesh_vel, inverse, rows):
    product = dot(space, operand(value))
    total = product[:rows]
    for d in range(3):
        total = total - mesh_vel[d : d + 1] * product[(d + 1) * rows : (d + 2) * rows]
    return total * inverse


def gather_trace(table, ones, faces, trace_op, rows, trace_rows, num_faces):
    found = dot(table, ones)
    high, low = found[:rows].astype(BF16), found[rows:].astype(BF16)
    every = dot(trace_op, jnp.concatenate([high, low, high], axis=0))
    trace = jnp.where(faces == 0, every[:trace_rows], 0.0)
    for k in range(1, num_faces):
        trace = trace + jnp.where(faces == k, every[k * trace_rows : (k + 1) * trace_rows], 0.0)
    return trace


def front_kernel(
    sizes,
    conserved_ref,
    size_ref,
    sound_ref,
    vertex_ref,
    share_ref,
    corner_ref,
    jac_ref,
    der_ref,
    res_ref,
    lift_ref,
    slab_elem_ref,
    slab_face_ref,
    peer_elem_ref,
    peer_face_ref,
    slab_normal_ref,
    peer_normal_ref,
    count_ref,
    sel_vt,
    sel_bt,
    sel_jac,
    sel_der,
    sel_res,
    sel_tvt,
    sel_tjac,
    sel_b,
    sel_lift,
    same_v,
    same_tv,
    same_f,
    same_vt,
    keep,
    table_ref,
    motion_ref,
    step_ref,
    own_ref,
    theirs_ref,
    inside_ref,
    trace_ref,
    flux_ref,
    lifting_ref,
    bound_index_ref,
    bound_values_ref,
    state,
    first,
    second,
    third,
    space_ref,
    ones,
    parts,
    jac,
    der,
    res,
    lift,
    vert_send,
    vert_recv,
    min_t,
    min_s,
    slab_send,
    slab_recv,
    peer_send,
    peer_recv,
    vert_sems,
    min_t_sems,
    min_s_sems,
    slab_sems,
    peer_sems,
):
    num_vars, basis, rows, trace_rows, num_faces, slabs, peers, chunk = sizes
    elems = conserved_ref.shape[2]
    shared = share_ref.shape[1]
    verts = vertex_ref.shape[1]
    slab_width = slab_send.shape[2]
    peer_width = peer_send.shape[2]
    send_rows = slab_send.shape[1]
    s = lax.axis_index("shock")
    t = lax.axis_index("trans")

    barrier = pltpu.get_barrier_semaphore()
    for o in range(1, peers):
        pl.semaphore_signal(
            barrier, inc=1, device_id=(s, lax.rem(t + o, peers)), device_id_type=MESH
        )
    for o in range(1, slabs):
        pl.semaphore_signal(
            barrier, inc=1, device_id=(lax.rem(s + o, slabs), t), device_id_type=MESH
        )

    def spread(velocity):
        high, low = split(velocity)
        rest = velocity - high.astype(F32) - low.astype(F32)
        return high.astype(F32), low.astype(F32), rest

    parts[...] = jnp.zeros_like(parts)
    for i, piece in enumerate(spread(vertex_ref[...])):
        parts[8 * i : 8 * i + 3, :verts] = piece
    share = jnp.concatenate([share_ref[0:1, :], share_ref[1:2, :]], axis=1)
    sent = dot(parts[:, :verts].astype(BF16), ones_at(share, verts))
    sent = sent[0:8] + sent[8:16] + sent[16:24]
    vert_send[0] = sent[:, :shared]
    vert_send[1] = sent[:, shared:]
    pl.semaphore_wait(barrier, peers - 1 + slabs - 1)

    def to_lower(source, dest, sems):
        return pltpu.make_async_remote_copy(
            src_ref=source.at[0],
            dst_ref=dest.at[1],
            send_sem=sems.at[0],
            recv_sem=sems.at[3],
            device_id=(s - 1, t),
            device_id_type=MESH,
        )

    def to_upper(source, dest, sems):
        return pltpu.make_async_remote_copy(
            src_ref=source.at[1],
            dst_ref=dest.at[0],
            send_sem=sems.at[1],
            recv_sem=sems.at[2],
            device_id=(s + 1, t),
            device_id_type=MESH,
        )

    def start_slab(source, dest, sems):
        @pl.when(s > 0)
        def _():
            to_lower(source, dest, sems).start()

        @pl.when(s < slabs - 1)
        def _():
            to_upper(source, dest, sems).start()

    def finish_slab(source, dest, sems):
        @pl.when(s > 0)
        def _():
            to_lower(source, dest, sems).wait_send()
            to_upper(source, dest, sems).wait_recv()

        @pl.when(s < slabs - 1)
        def _():
            to_upper(source, dest, sems).wait_send()
            to_lower(source, dest, sems).wait_recv()

        @pl.when(s == 0)
        def _():
            dest[0] = jnp.zeros(dest.shape[1:], F32)

        @pl.when(s == slabs - 1)
        def _():
            dest[1] = jnp.zeros(dest.shape[1:], F32)

    start_slab(vert_send, vert_recv, vert_sems)

    for small, held in ((jac_ref, jac), (der_ref, der), (res_ref, res), (lift_ref, lift)):
        count = small.shape[1]
        for i in range(small.shape[0]):
            held[i * count : (i + 1) * count, :] = small[i]
    jac_wide = exact(sel_jac[...], exact(jac[...], sel_vt[...]))
    der_wide = exact(sel_der[...], exact(der[...], sel_bt[...]))
    both = jac_wide * der_wide
    space_ref[0:rows, :] = operator(both[:rows] + both[rows : 2 * rows] + both[2 * rows :])
    for d in range(3):
        space_ref[(d + 1) * rows : (d + 2) * rows, :] = operator(
            der_wide[d * rows : (d + 1) * rows] * same_v[...]
        )
    for b in range(basis):
        state[b * num_vars : (b + 1) * num_vars, :] = conserved_ref[b]
    state[num_vars * basis :, :] = jnp.zeros((rows - num_vars * basis, elems), F32)

    def counted(columns, low, count):
        places = lax.broadcasted_iota(jnp.int32, (count, chunk), 0) + low
        total = jnp.where(places == corner_ref[0:1, columns], 1.0, 0.0)
        for i in range(1, 4):
            total = total + jnp.where(places == corner_ref[i : i + 1, columns], 1.0, 0.0)
        return total.astype(BF16)

    own_parts = parts[:, :verts].astype(BF16)

    def own_corner(c, carry):
        columns = pl.ds(pl.multiple_of(c * chunk, chunk), chunk)
        found = dot(own_parts, counted(columns, 0, verts))
        motion_ref[:, columns] = found[0:8] + found[8:16] + found[16:24]
        return carry

    lax.fori_loop(0, elems // chunk, own_corner, 0)
    finish_slab(vert_send, vert_recv, vert_sems)
    for side in range(2):
        place = verts + side * shared
        for i, piece in enumerate(spread(vert_recv[side])):
            parts[8 * i : 8 * i + 8, place : place + shared] = piece
    far_parts = parts[:, verts:].astype(BF16)

    def far_corner(c, smallest):
        columns = pl.ds(pl.multiple_of(c * chunk, chunk), chunk)
        found = dot(far_parts, counted(columns, verts, 2 * shared))
        vel = 0.25 * (motion_ref[:, columns] + (found[0:8] + found[8:16] + found[16:24]))
        size = size_ref[0:1, columns]
        speed = (
            sound_ref[0:1, columns] + jnp.abs(vel[0:1]) + jnp.abs(vel[1:2]) + jnp.abs(vel[2:3])
        )
        motion_ref[0:3, columns] = vel[0:3]
        motion_ref[3:4, columns] = 1.0 / size
        motion_ref[4:5, columns] = speed
        return jnp.minimum(smallest, jnp.min(size / speed, axis=1, keepdims=True))

    smallest = lax.fori_loop(0, elems // chunk, far_corner, jnp.full((1, 1), jnp.inf, F32))

    def min_copy(buffer, sems, place, count, o, along_trans):
        to = lax.rem(place + o, count)
        return pltpu.make_async_remote_copy(
            src_ref=buffer.at[place],
            dst_ref=buffer.at[place],
            send_sem=sems.at[0, o],
            recv_sem=sems.at[1, place],
            device_id=(s, to) if along_trans else (to, t),
            device_id_type=MESH,
        )

    def min_wait(buffer, sems, place, count, along_trans):
        for o in range(1, count):
            origin = lax.rem(place + count - o, count)
            pltpu.make_async_remote_copy(
                src_ref=buffer.at[origin],
                dst_ref=buffer.at[origin],
                send_sem=sems.at[0, o],
                recv_sem=sems.at[1, origin],
                device_id=(s, origin) if along_trans else (origin, t),
                device_id_type=MESH,
            ).wait_recv()
            min_copy(buffer, sems, place, count, o, along_trans).wait_send()

    min_t[t] = jnp.broadcast_to(smallest, min_t.shape[1:])
    for o in range(1, peers):
        min_copy(min_t, min_t_sems, t, peers, o, True).start()

    def space_step(source, dest):
        for c in range(elems // chunk):
            columns = pl.ds(c * chunk, chunk)
            dest[:, columns] = apply_space(
                space_ref[...],
                source[:, columns],
                motion_ref[:, columns],
                motion_ref[3:4, columns],
                rows,
            )

    space_step(state, first)
    min_wait(min_t, min_t_sems, t, peers, True)
    best = min_t[0]
    for i in range(1, peers):
        best = jnp.minimum(best, min_t[i])
    min_s[s] = best
    for o in range(1, slabs):
        min_copy(min_s, min_s_sems, s, slabs, o, False).start()
    space_step(first, second)
    space_step(second, third)

    res_wide = exact(sel_res[...], exact(res[...], sel_bt[...]))
    for k in range(num_faces):
        trace_ref[k * trace_rows : (k + 1) * trace_rows, :] = operator(
            res_wide[k * trace_rows : (k + 1) * trace_rows] * same_tv[...] + keep[...]
        )
    tjac_wide = exact(sel_tjac[...], exact(jac[...], sel_tvt[...]))
    for d in range(3):
        flux_ref[d * trace_rows : (d + 1) * trace_rows, :] = operator(
            tjac_wide[d * trace_rows : (d + 1) * trace_rows] * same_f[...]
        )
    lift_rows = lax.dot_general(
        sel_b[...],
        lift[...],
        (((1,), (1,)), ((), ())),
        precision=lax.Precision.HIGHEST,
        preferred_element_type=F32,
    )
    lift_wide = exact(lift_rows, sel_lift[...])
    spread_v = jnp.concatenate([same_vt[...]] * num_faces, axis=1)
    lifting_ref[...] = operator(lift_wide * spread_v)
    for row, slab_ref, peer_ref in (
        (0, slab_elem_ref, peer_elem_ref),
        (1, slab_face_ref, peer_face_ref),
    ):
        for side in range(2):
            bound_index_ref[row : row + 1, side * slab_width : (side + 1) * slab_width] = slab_ref[
                side : side + 1, :
            ]
        for q in range(peers):
            low_end = 2 * slab_width + q * peer_width
            bound_index_ref[row : row + 1, low_end : low_end + peer_width] = peer_ref[
                q : q + 1, :
            ]
    for d in range(3):
        for side in range(2):
            bound_values_ref[d : d + 1, side * slab_width : (side + 1) * slab_width] = (
                slab_normal_ref[d, side : side + 1, :]
            )
        for q in range(peers):
            low_end = 2 * slab_width + q * peer_width
            bound_values_ref[d : d + 1, low_end : low_end + peer_width] = peer_normal_ref[
                d, q : q + 1, :
            ]
    bound_values_ref[3:4, : 2 * slab_width] = jnp.ones((1, 2 * slab_width), F32)
    slot = lax.broadcasted_iota(jnp.int32, (1, peer_width), 1)
    for q in range(peers):
        low_end = 2 * slab_width + q * peer_width
        bound_values_ref[3:4, low_end : low_end + peer_width] = jnp.where(
            slot < count_ref[0:1, q : q + 1], 1.0, 0.0
        )
    ones[...] = ones_at(bound_index_ref[0:1, :], elems)

    min_wait(min_s, min_s_sems, s, slabs, False)
    best = min_s[0]
    for i in range(1, slabs):
        best = jnp.minimum(best, min_s[i])
    step = CFL_NUMBER * best
    step_ref[...] = step
    dt = step[0:1, 0:1]
    table_ref[...] = (
        state[...] - (0.5 * dt) * first[...] + (dt * dt * (1.0 / 6.0)) * second[...]
    )
    inside_ref[...] = (
        first[...] - (0.5 * dt) * second[...] + (dt * dt * (1.0 / 6.0)) * third[...]
    )
    flat = num_vars * basis
    table_ref[flat : flat + 1, :] = motion_ref[4:5, :]
    high, low = split(table_ref[...])
    trace = gather_trace(
        jnp.concatenate([high, low], axis=0),
        ones[...],
        bound_index_ref[1:2, :],
        trace_ref[...],
        rows,
        trace_rows,
        num_faces,
    )
    own_ref[...] = trace
    cut = trace[:send_rows]
    slab_send[0] = cut[:, :slab_width]
    slab_send[1] = cut[:, slab_width : 2 * slab_width]
    for q in range(peers):
        low_end = 2 * slab_width + q * peer_width
        peer_send[q] = cut[:, low_end : low_end + peer_width]
    start_slab(slab_send, slab_recv, slab_sems)

    def peer_copy(o):
        to = lax.rem(t + o, peers)
        return pltpu.make_async_remote_copy(
            src_ref=peer_send.at[to],
            dst_ref=peer_recv.at[t],
            send_sem=peer_sems.at[0, o],
            recv_sem=peer_sems.at[1, t],
            device_id=(s, to),
            device_id_type=MESH,
        )

    for o in range(1, peers):
        peer_copy(o).start()
    peer_recv[t] = jnp.zeros(peer_recv.shape[1:], F32)
    theirs_ref[...] = jnp.zeros_like(theirs_ref)
    for o in range(1, peers):
        peer_copy(o).wait_send()
        origin = lax.rem(t + peers - o, peers)
        pltpu.make_async_remote_copy(
            src_ref=peer_send.at[origin],
            dst_ref=peer_recv.at[origin],
            send_sem=peer_sems.at[0, o],
            recv_sem=peer_sems.at[1, origin],
            device_id=(s, origin),
            device_id_type=MESH,
        ).wait_recv()
    for q in range(peers):
        low_end = 2 * slab_width + q * peer_width
        theirs_ref[:send_rows, low_end : low_end + peer_width] = peer_recv[q]
    finish_slab(slab_send, slab_recv, slab_sems)
    for side in range(2):
        theirs_ref[:send_rows, side * slab_width : (side + 1) * slab_width] = slab_recv[side]


def back_kernel(
    sizes,
    table_ref,
    motion_ref,
    own_ref,
    theirs_ref,
    inside_ref,
    trace_ref,
    flux_ref,
    lifting_ref,
    bound_index_ref,
    bound_values_ref,
    inner_elem_ref,
    inner_face_ref,
    inner_normal_ref,
    step_ref,
    rate_ref,
    step_out_ref,
    table,
    ones_0,
    ones_1,
    ones_2,
    pair_0,
    pair_1,
    ones_bound,
    total,
):
    num_vars, basis, rows, trace_rows, num_faces, flat_trace, chunk, tile, part = sizes
    elems = table_ref.shape[1]
    lift_rows = lifting_ref.shape[0]
    all_ones, all_pairs = (ones_0, ones_1, ones_2), (pair_0, pair_1)
    tiles, pieces = inner_elem_ref.shape[1] // tile, tile // part
    step_out_ref[0, 0] = step_ref[0, 0]
    high, low = split(table_ref[...])
    table[:rows, :] = high
    table[rows:, :] = low

    def normal_flux(jump, normal):
        product = dot(flux_ref[...], operand(jump))
        result = normal[0:1] * product[:trace_rows]
        for d in range(1, 3):
            result = result + normal[d : d + 1] * product[d * trace_rows : (d + 1) * trace_rows]
        return result

    def lifted(flux, faces):
        high = flux.astype(BF16).astype(F32)
        low = flux - high
        highs = [jnp.where(faces == k, high, 0.0).astype(BF16) for k in range(num_faces)]
        lows = [jnp.where(faces == k, low, 0.0).astype(BF16) for k in range(num_faces)]
        value = dot(lifting_ref[...], jnp.concatenate(highs + lows + highs, axis=0))
        return jnp.concatenate(split(value), axis=0)

    def scatter(where_ones, pair, lines):
        return lax.dot_general(
            where_ones[lines, :],
            pair,
            (((1,), (1,)), ((), ())),
            preferred_element_type=F32,
        )

    def both_sides(ref, j, c):
        columns = pl.ds(j * tile + c * part, part)
        return jnp.concatenate([ref[0:1, columns], ref[1:2, columns]], axis=1)

    def build(j, c):
        all_ones[j % 3][:, 2 * part * c : 2 * part * (c + 1)] = ones_at(
            both_sides(inner_elem_ref, j, c), elems
        )

    def chain(j, c):
        face = both_sides(inner_face_ref, j, c)
        columns = slice(2 * part * c, 2 * part * (c + 1))
        trace = gather_trace(
            table[...],
            all_ones[j % 3][:, columns],
            face,
            trace_ref[...],
            rows,
            trace_rows,
            num_faces,
        )
        jump = trace[:, part:] - trace[:, :part]
        bound = jnp.maximum(
            trace[flat_trace : flat_trace + 1, :part], trace[flat_trace : flat_trace + 1, part:]
        )
        flow = normal_flux(jump, inner_normal_ref[:, pl.ds(j * tile + c * part, part)])
        drop = bound * jump
        flux = 0.5 * jnp.concatenate([flow - drop, flow + drop], axis=1)
        all_pairs[j % 2][:, columns] = lifted(flux, face)

    def lines_of(c):
        return slice(c * (elems // pieces), (c + 1) * (elems // pieces))

    for c in range(pieces):
        build(0, c)
    ones_bound[...] = ones_at(bound_index_ref[0:1, :], elems)
    own, theirs = own_ref[...], theirs_ref[...]
    jump = theirs - own
    bound = jnp.maximum(
        own[flat_trace : flat_trace + 1, :], theirs[flat_trace : flat_trace + 1, :]
    )
    flux = normal_flux(jump, bound_values_ref[...]) - bound * jump
    bound_pair = lifted((0.5 * bound_values_ref[3:4, :]) * flux, bound_index_ref[1:2, :])

    for j in range(tiles):
        for c in range(pieces):
            lines = lines_of(c)
            if j + 1 < tiles:
                build(j + 1, c)
            chain(j, c)
            if j == 0:
                total[lines, :] = scatter(ones_bound, bound_pair, lines)
            else:
                total[lines, :] += scatter(
                    all_ones[(j - 1) % 3], all_pairs[(j - 1) % 2][...], lines
                )
    for c in range(pieces):
        lines = lines_of(c)
        last = total[lines, :] + scatter(
            all_ones[(tiles - 1) % 3], all_pairs[(tiles - 1) % 2][...], lines
        )
        face_term = jnp.transpose(last[:, :lift_rows] + last[:, lift_rows:])
        rate = -(inside_ref[:, lines] + face_term[:rows] * motion_ref[3:4, lines])
        for b in range(basis):
            rate_ref[b, :, lines] = rate[b * num_vars : (b + 1) * num_vars]


def body(
    conserved,
    cell_size,
    sound_speed,
    jacobian,
    derivative,
    restriction,
    lifting,
    vertex_velocity,
    share_index,
    elem_vertex,
    inner_elem,
    inner_face,
    inner_normal,
    slab_elem,
    slab_face,
    slab_normal,
    peer_elem,
    peer_face,
    peer_normal,
    peer_count,
):
    num_vars, basis, elems = conserved.shape
    num_faces, face_basis = restriction.shape[:2]
    slabs, peers = lax.axis_size("shock"), lax.axis_size("trans")
    slab_width, peer_width = slab_elem.shape[1], peer_elem.shape[1]
    verts, shared = vertex_velocity.shape[1], share_index.shape[1]
    rows = up_to(num_vars * basis + 1, 16)
    lift_rows = up_to(rows, 128)
    flat_trace = num_vars * face_basis
    trace_rows = up_to(flat_trace + 1, 16)
    send_rows = up_to(flat_trace + 1, 8)
    sides = 2 * slab_width + peers * peer_width
    chunk = min(512, elems)
    part = min(128, inner_elem.shape[1])
    tile = min(4 * part, inner_elem.shape[1])

    spreads = [
        jnp.asarray(a)
        for a in selections(num_vars, basis, face_basis, num_faces, rows, lift_rows, trace_rows)
    ]
    vmem = pl.BlockSpec(memory_space=pltpu.VMEM)
    out_shapes = (
        jax.ShapeDtypeStruct((rows, elems), F32),
        jax.ShapeDtypeStruct((8, elems), F32),
        jax.ShapeDtypeStruct((8, 128), F32),
        jax.ShapeDtypeStruct((trace_rows, sides), F32),
        jax.ShapeDtypeStruct((trace_rows, sides), F32),
        jax.ShapeDtypeStruct((rows, elems), F32),
        jax.ShapeDtypeStruct((num_faces * trace_rows, 3 * rows), BF16),
        jax.ShapeDtypeStruct((3 * trace_rows, 3 * trace_rows), BF16),
        jax.ShapeDtypeStruct((lift_rows, 3 * num_faces * trace_rows), BF16),
        jax.ShapeDtypeStruct((2, sides), jnp.int32),
        jax.ShapeDtypeStruct((4, sides), F32),
    )
    front_args = [
        jnp.transpose(conserved, (1, 0, 2)),
        cell_size.reshape(1, elems),
        sound_speed.reshape(1, elems),
        vertex_velocity,
        share_index,
        elem_vertex,
        jnp.transpose(jacobian, (1, 0, 2)),
        jnp.transpose(derivative, (1, 0, 2)),
        jnp.transpose(restriction, (1, 0, 2)),
        jnp.transpose(lifting, (2, 0, 1)),
        slab_elem,
        slab_face,
        peer_elem,
        peer_face,
        slab_normal,
        peer_normal,
        jnp.transpose(peer_count),
        *spreads,
    ]
    dma = pltpu.SemaphoreType.DMA
    table, motion, step, own, theirs, inside, trace, flux, lift, bound_index, bound_values = pl.pallas_call(
        functools.partial(
            front_kernel,
            (num_vars, basis, rows, trace_rows, num_faces, slabs, peers, chunk),
        ),
        out_shape=out_shapes,
        in_specs=[vmem] * len(front_args),
        out_specs=[vmem] * len(out_shapes),
        scratch_shapes=[
            pltpu.VMEM((rows, elems), F32),
            pltpu.VMEM((rows, elems), F32),
            pltpu.VMEM((rows, elems), F32),
            pltpu.VMEM((rows, elems), F32),
            pltpu.VMEM((4 * rows, 3 * rows), BF16),
            pltpu.VMEM((elems, sides), BF16),
            pltpu.VMEM((24, verts + 2 * shared), F32),
            pltpu.VMEM((3 * num_vars, num_vars), F32),
            pltpu.VMEM((3 * basis, basis), F32),
            pltpu.VMEM((num_faces * face_basis, basis), F32),
            pltpu.VMEM((num_faces * face_basis, basis), F32),
            pltpu.VMEM((2, 8, shared), F32),
            pltpu.VMEM((2, 8, shared), F32),
            pltpu.VMEM((peers, 8, 128), F32),
            pltpu.VMEM((slabs, 8, 128), F32),
            pltpu.VMEM((2, send_rows, slab_width), F32),
            pltpu.VMEM((2, send_rows, slab_width), F32),
            pltpu.VMEM((peers, send_rows, peer_width), F32),
            pltpu.VMEM((peers, send_rows, peer_width), F32),
            dma((4,)),
            dma((2, peers)),
            dma((2, slabs)),
            dma((4,)),
            dma((2, peers)),
        ],
        compiler_params=pltpu.CompilerParams(
            collective_id=0, has_side_effects=True, vmem_limit_bytes=VMEM_BYTES
        ),
        name="front",
    )(*front_args)

    back_args = [
        table,
        motion,
        own,
        theirs,
        inside,
        trace,
        flux,
        lift,
        bound_index,
        bound_values,
        inner_elem,
        inner_face,
        inner_normal,
        step,
    ]
    rate, step = pl.pallas_call(
        functools.partial(
            back_kernel,
            (num_vars, basis, rows, trace_rows, num_faces, flat_trace, chunk, tile, part),
        ),
        out_shape=(
            jax.ShapeDtypeStruct((basis, num_vars, elems), F32),
            jax.ShapeDtypeStruct((1, 1), F32),
        ),
        in_specs=[vmem] * (len(back_args) - 1) + [pl.BlockSpec(memory_space=pltpu.SMEM)],
        out_specs=(vmem, pl.BlockSpec(memory_space=pltpu.SMEM)),
        scratch_shapes=[
            pltpu.VMEM((2 * rows, elems), BF16),
            pltpu.VMEM((elems, 2 * tile), BF16),
            pltpu.VMEM((elems, 2 * tile), BF16),
            pltpu.VMEM((elems, 2 * tile), BF16),
            pltpu.VMEM((2 * lift_rows, 2 * tile), BF16),
            pltpu.VMEM((2 * lift_rows, 2 * tile), BF16),
            pltpu.VMEM((elems, sides), BF16),
            pltpu.VMEM((elems, 2 * lift_rows), F32),
        ],
        compiler_params=pltpu.CompilerParams(vmem_limit_bytes=VMEM_BYTES),
        name="back",
    )(*back_args)
    return jnp.transpose(rate, (1, 0, 2)), step.reshape(())


def solution(mesh):
    both = ("shock", "trans")
    last2, last3 = P(None, both), P(None, None, both)
    return jax.shard_map(
        body,
        mesh=mesh,
        in_specs=(
            last3,
            P(both),
            P(both),
            P(),
            P(),
            P(),
            P(),
            last2,
            last2,
            last2,
            last2,
            last2,
            last2,
            last2,
            last2,
            last3,
            last2,
            last2,
            last3,
            last2,
        ),
        out_specs=(last3, P()),
        check_vma=False,
    )
```

```python
import functools

import jax
import jax.numpy as jnp
import numpy as np
from jax import lax
from jax.experimental import pallas as pl
from jax.experimental.pallas import tpu as pltpu
from jax.sharding import PartitionSpec as P

CFL_NUMBER = 0.3
F32 = jnp.float32
BF16 = jnp.bfloat16
MESH = pl.DeviceIdType.MESH
VMEM_BYTES = 56 * 1024 * 1024


def up_to(value, multiple):
    return -(-value // multiple) * multiple


def selections(num_vars, basis, face_basis, faces, rows, lift_rows, trace_rows):
    flat, flat_t = num_vars * basis, num_vars * face_basis
    row, trow = np.arange(rows), np.arange(trace_rows)
    row_v, row_b = (
        np.where(row < flat, row % num_vars, -1),
        np.where(row < flat, row // num_vars, -1),
    )
    lift_v, lift_b = (
        np.pad(a, (0, lift_rows - rows), constant_values=-1) for a in (row_v, row_b)
    )
    trow_v = np.where(trow < flat_t, trow // face_basis, -2)
    trow_f = np.where(trow < flat_t, trow % face_basis, -2)

    def pick(target, count):
        return (target[:, None] == np.arange(count)[None, :]).astype(np.float32)

    def block(target, count, copies):
        out = np.zeros((copies, target.size, copies * count), np.float32)
        for k in range(copies):
            out[k, :, k::copies] = pick(target, count)
        return out.reshape(copies * target.size, copies * count)

    same_v = (row_v[:, None] == row_v[None, :]) & (row_v[:, None] >= 0)
    same_vt = (lift_v[:, None] == trow_v[None, :]) & (lift_v[:, None] >= 0)
    same_tv = (trow_v[:, None] == row_v[None, :]) & (trow_v[:, None] >= 0)
    same_f = (trow_f[:, None] == trow_f[None, :]) & (trow_f[:, None] >= 0)
    keep = np.zeros((trace_rows, rows), np.float32)
    keep[flat_t, flat] = 1.0
    return [
        np.ascontiguousarray(pick(row_v, num_vars).T),
        np.ascontiguousarray(pick(row_b, basis).T),
        block(row_v, num_vars, 3),
        block(row_b, basis, 3),
        block(trow_f, face_basis, faces),
        np.ascontiguousarray(pick(trow_v, num_vars).T),
        block(trow_v, num_vars, 3),
        pick(lift_b, basis),
        np.ascontiguousarray(block(trow_f, face_basis, faces).T),
        same_v.astype(np.float32),
        same_tv.astype(np.float32),
        same_f.astype(np.float32),
        same_vt.astype(np.float32),
        keep,
    ]


def exact(a, b):
    return jnp.dot(a, b, precision=lax.Precision.HIGHEST, preferred_element_type=F32)


def dot(a, b):
    return jnp.dot(a, b, preferred_element_type=F32)


def split(value):
    high = value.astype(BF16)
    return high, (value - high.astype(F32)).astype(BF16)


def operator(matrix):
    high, low = split(matrix)
    return jnp.concatenate([high, high, low], axis=1)


def operand(value):
    high, low = split(value)
    return jnp.concatenate([high, low, high], axis=0)


def fill_ones(dest, line, lines, index_of, width):
    deep, wide = min(32, lines), min(256, width)
    places = lax.broadcasted_iota(jnp.int32, (deep, wide), 0)
    for column in range(0, width, wide):
        index = index_of(column, wide) - line
        for row in range(0, lines, deep):
            block = jnp.where(places == index - row, 1.0, 0.0).astype(BF16)
            at = pl.ds(pl.multiple_of(line + row, deep), deep)
            dest[at, column : column + wide] = block


def in_steps(count, step, work):
    def one(i, carry):
        work(pl.multiple_of(i * step, step))
        return carry

    lax.fori_loop(0, count // step, one, 0)


def apply_space(space, value, mesh_vel, inverse, rows):
    product = dot(space, operand(value))
    total = product[:rows]
    for d in range(3):
        total = total - mesh_vel[d : d + 1] * product[(d + 1) * rows : (d + 2) * rows]
    return total * inverse


def gather_trace(table, ones, faces, trace_op, rows, trace_rows, num_faces):
    found = dot(table, ones)
    high, low = found[:rows].astype(BF16), found[rows:].astype(BF16)
    every = dot(trace_op, jnp.concatenate([high, low, high], axis=0))
    trace = jnp.where(faces == 0, every[:trace_rows], 0.0)
    for k in range(1, num_faces):
        trace = trace + jnp.where(faces == k, every[k * trace_rows : (k + 1) * trace_rows], 0.0)
    return trace


def front_kernel(
    sizes,
    conserved_ref,
    size_ref,
    sound_ref,
    vertex_ref,
    share_ref,
    corner_ref,
    jac_ref,
    der_ref,
    res_ref,
    lift_ref,
    slab_elem_ref,
    slab_face_ref,
    peer_elem_ref,
    peer_face_ref,
    slab_normal_ref,
    peer_normal_ref,
    count_ref,
    sel_vt,
    sel_bt,
    sel_jac,
    sel_der,
    sel_res,
    sel_tvt,
    sel_tjac,
    sel_b,
    sel_lift,
    same_v,
    same_tv,
    same_f,
    same_vt,
    keep,
    table_ref,
    motion_ref,
    step_ref,
    own_ref,
    theirs_ref,
    inside_ref,
    trace_ref,
    flux_ref,
    lifting_ref,
    bound_index_ref,
    bound_values_ref,
    state,
    first,
    second,
    third,
    space_ref,
    ones,
    counts,
    parts,
    jac,
    der,
    res,
    lift,
    vert_send,
    vert_recv,
    min_t,
    min_s,
    slab_send,
    slab_recv,
    peer_send,
    peer_recv,
    vert_sems,
    min_t_sems,
    min_s_sems,
    slab_sems,
    peer_sems,
):
    num_vars, basis, rows, trace_rows, num_faces, slabs, peers, chunk = sizes
    elems = conserved_ref.shape[2]
    shared = share_ref.shape[1]
    verts = vertex_ref.shape[1]
    slab_width = slab_send.shape[2]
    peer_width = peer_send.shape[2]
    send_rows = slab_send.shape[1]
    s = lax.axis_index("shock")
    t = lax.axis_index("trans")

    barrier = pltpu.get_barrier_semaphore()
    for o in range(1, peers):
        pl.semaphore_signal(
            barrier, inc=1, device_id=(s, lax.rem(t + o, peers)), device_id_type=MESH
        )
    for o in range(1, slabs):
        pl.semaphore_signal(
            barrier, inc=1, device_id=(lax.rem(s + o, slabs), t), device_id_type=MESH
        )

    def spread(velocity):
        high, low = split(velocity)
        rest = velocity - high.astype(F32) - low.astype(F32)
        return high.astype(F32), low.astype(F32), rest

    parts[...] = jnp.zeros_like(parts)
    for i, piece in enumerate(spread(vertex_ref[...])):
        parts[8 * i : 8 * i + 3, :verts] = piece
    share = jnp.concatenate([share_ref[0:1, :], share_ref[1:2, :]], axis=1)
    places = lax.broadcasted_iota(jnp.int32, (verts, 2 * shared), 0)
    sent = dot(
        parts[:, :verts].astype(BF16), jnp.where(places == share, 1.0, 0.0).astype(BF16)
    )
    sent = sent[0:8] + sent[8:16] + sent[16:24]
    vert_send[0] = sent[:, :shared]
    vert_send[1] = sent[:, shared:]
    pl.semaphore_wait(barrier, peers - 1 + slabs - 1)

    def to_lower(source, dest, sems):
        return pltpu.make_async_remote_copy(
            src_ref=source.at[0],
            dst_ref=dest.at[1],
            send_sem=sems.at[0],
            recv_sem=sems.at[3],
            device_id=(s - 1, t),
            device_id_type=MESH,
        )

    def to_upper(source, dest, sems):
        return pltpu.make_async_remote_copy(
            src_ref=source.at[1],
            dst_ref=dest.at[0],
            send_sem=sems.at[1],
            recv_sem=sems.at[2],
            device_id=(s + 1, t),
            device_id_type=MESH,
        )

    def start_slab(source, dest, sems):
        @pl.when(s > 0)
        def _():
            to_lower(source, dest, sems).start()

        @pl.when(s < slabs - 1)
        def _():
            to_upper(source, dest, sems).start()

    def finish_slab(source, dest, sems):
        @pl.when(s > 0)
        def _():
            to_lower(source, dest, sems).wait_send()
            to_upper(source, dest, sems).wait_recv()

        @pl.when(s < slabs - 1)
        def _():
            to_upper(source, dest, sems).wait_send()
            to_lower(source, dest, sems).wait_recv()

        @pl.when(s == 0)
        def _():
            dest[0] = jnp.zeros(dest.shape[1:], F32)

        @pl.when(s == slabs - 1)
        def _():
            dest[1] = jnp.zeros(dest.shape[1:], F32)

    start_slab(vert_send, vert_recv, vert_sems)

    for small, held in ((jac_ref, jac), (der_ref, der), (res_ref, res), (lift_ref, lift)):
        count = small.shape[1]
        for i in range(small.shape[0]):
            held[i * count : (i + 1) * count, :] = small[i]
    jac_wide = exact(sel_jac[...], exact(jac[...], sel_vt[...]))
    der_wide = exact(sel_der[...], exact(der[...], sel_bt[...]))
    both = jac_wide * der_wide
    space_ref[0:rows, :] = operator(both[:rows] + both[rows : 2 * rows] + both[2 * rows :])
    for d in range(3):
        space_ref[(d + 1) * rows : (d + 2) * rows, :] = operator(
            der_wide[d * rows : (d + 1) * rows] * same_v[...]
        )
    for b in range(basis):
        state[b * num_vars : (b + 1) * num_vars, :] = conserved_ref[b]
    state[num_vars * basis :, :] = jnp.zeros((rows - num_vars * basis, elems), F32)

    deep, wide = 32, min(256, elems)
    places = lax.broadcasted_iota(jnp.int32, (deep, wide), 0)

    def count_corners(line):
        for column in range(0, elems, wide):
            total = jnp.zeros((deep, wide), F32)
            for i in range(4):
                index = corner_ref[i : i + 1, column : column + wide] - line
                total = total + jnp.where(places == index, 1.0, 0.0)
            counts[pl.ds(line, deep), column : column + wide] = total.astype(BF16)

    in_steps(verts + 2 * shared, deep, count_corners)
    finish_slab(vert_send, vert_recv, vert_sems)
    for side in range(2):
        place = verts + side * shared
        for i, piece in enumerate(spread(vert_recv[side])):
            parts[8 * i : 8 * i + 8, place : place + shared] = piece
    all_parts = parts[...].astype(BF16)
    smallest = jnp.full((1, 1), jnp.inf, F32)
    for column in range(0, elems, chunk):
        columns = slice(column, column + chunk)
        found = dot(all_parts, counts[:, columns])
        vel = 0.25 * (found[0:8] + found[8:16] + found[16:24])
        size = size_ref[0:1, columns]
        speed = (
            sound_ref[0:1, columns] + jnp.abs(vel[0:1]) + jnp.abs(vel[1:2]) + jnp.abs(vel[2:3])
        )
        motion_ref[0:3, columns] = vel[0:3]
        motion_ref[3:4, columns] = 1.0 / size
        motion_ref[4:8, columns] = jnp.broadcast_to(speed, (4, chunk))
        smallest = jnp.minimum(smallest, jnp.min(size / speed, axis=1, keepdims=True))

    def min_copy(buffer, sems, place, count, o, along_trans):
        to = lax.rem(place + o, count)
        return pltpu.make_async_remote_copy(
            src_ref=buffer.at[place],
            dst_ref=buffer.at[place],
            send_sem=sems.at[0, o],
            recv_sem=sems.at[1, place],
            device_id=(s, to) if along_trans else (to, t),
            device_id_type=MESH,
        )

    def min_wait(buffer, sems, place, count, along_trans):
        for o in range(1, count):
            origin = lax.rem(place + count - o, count)
            pltpu.make_async_remote_copy(
                src_ref=buffer.at[origin],
                dst_ref=buffer.at[origin],
                send_sem=sems.at[0, o],
                recv_sem=sems.at[1, origin],
                device_id=(s, origin) if along_trans else (origin, t),
                device_id_type=MESH,
            ).wait_recv()
            min_copy(buffer, sems, place, count, o, along_trans).wait_send()

    min_t[t] = jnp.broadcast_to(smallest, min_t.shape[1:])
    for o in range(1, peers):
        min_copy(min_t, min_t_sems, t, peers, o, True).start()

    def space_step(source, dest):
        def one(column):
            columns = pl.ds(column, wide)
            dest[:, columns] = apply_space(
                space_ref[...],
                source[:, columns],
                motion_ref[:, columns],
                motion_ref[3:4, columns],
                rows,
            )

        in_steps(elems, wide, one)

    space_step(state, first)
    min_wait(min_t, min_t_sems, t, peers, True)
    best = min_t[0]
    for i in range(1, peers):
        best = jnp.minimum(best, min_t[i])
    min_s[s] = best
    for o in range(1, slabs):
        min_copy(min_s, min_s_sems, s, slabs, o, False).start()
    space_step(first, second)
    space_step(second, third)

    res_wide = exact(sel_res[...], exact(res[...], sel_bt[...]))
    for k in range(num_faces):
        trace_ref[k * trace_rows : (k + 1) * trace_rows, :] = operator(
            res_wide[k * trace_rows : (k + 1) * trace_rows] * same_tv[...] + keep[...]
        )
    tjac_wide = exact(sel_tjac[...], exact(jac[...], sel_tvt[...]))
    for d in range(3):
        flux_ref[d * trace_rows : (d + 1) * trace_rows, :] = operator(
            tjac_wide[d * trace_rows : (d + 1) * trace_rows] * same_f[...]
        )
    lift_rows = lax.dot_general(
        sel_b[...],
        lift[...],
        (((1,), (1,)), ((), ())),
        precision=lax.Precision.HIGHEST,
        preferred_element_type=F32,
    )
    lift_wide = exact(lift_rows, sel_lift[...])
    spread_v = jnp.concatenate([same_vt[...]] * num_faces, axis=1)
    lifting_ref[...] = operator(lift_wide * spread_v)
    for row, slab_ref, peer_ref in (
        (0, slab_elem_ref, peer_elem_ref),
        (1, slab_face_ref, peer_face_ref),
    ):
        for side in range(2):
            bound_index_ref[row : row + 1, side * slab_width : (side + 1) * slab_width] = slab_ref[
                side : side + 1, :
            ]
        for q in range(peers):
            low_end = 2 * slab_width + q * peer_width
            bound_index_ref[row : row + 1, low_end : low_end + peer_width] = peer_ref[
                q : q + 1, :
            ]
    for d in range(3):
        for side in range(2):
            bound_values_ref[d : d + 1, side * slab_width : (side + 1) * slab_width] = (
                slab_normal_ref[d, side : side + 1, :]
            )
        for q in range(peers):
            low_end = 2 * slab_width + q * peer_width
            bound_values_ref[d : d + 1, low_end : low_end + peer_width] = peer_normal_ref[
                d, q : q + 1, :
            ]
    bound_values_ref[3:4, : 2 * slab_width] = jnp.ones((1, 2 * slab_width), F32)
    slot = lax.broadcasted_iota(jnp.int32, (1, peer_width), 1)
    for q in range(peers):
        low_end = 2 * slab_width + q * peer_width
        bound_values_ref[3:4, low_end : low_end + peer_width] = jnp.where(
            slot < count_ref[0:1, q : q + 1], 1.0, 0.0
        )
    in_steps(
        elems,
        64,
        lambda line: fill_ones(
            ones, line, 64, lambda at, wide: bound_index_ref[0:1, at : at + wide], ones.shape[1]
        ),
    )

    min_wait(min_s, min_s_sems, s, slabs, False)
    best = min_s[0]
    for i in range(1, slabs):
        best = jnp.minimum(best, min_s[i])
    step = CFL_NUMBER * best
    step_ref[...] = step
    dt = step[0:1, 0:1]
    table_ref[...] = (
        state[...] - (0.5 * dt) * first[...] + (dt * dt * (1.0 / 6.0)) * second[...]
    )
    inside_ref[...] = (
        first[...] - (0.5 * dt) * second[...] + (dt * dt * (1.0 / 6.0)) * third[...]
    )
    flat = num_vars * basis
    table_ref[flat : flat + 1, :] = motion_ref[4:5, :]
    high, low = split(table_ref[...])
    pair = jnp.concatenate([high, low], axis=0)
    for column in range(0, ones.shape[1], wide):
        columns = slice(column, column + wide)
        own_ref[:, columns] = gather_trace(
            pair,
            ones[:, columns],
            bound_index_ref[1:2, columns],
            trace_ref[...],
            rows,
            trace_rows,
            num_faces,
        )
    slab_send[0] = own_ref[:send_rows, :slab_width]
    slab_send[1] = own_ref[:send_rows, slab_width : 2 * slab_width]
    for q in range(peers):
        low_end = 2 * slab_width + q * peer_width
        peer_send[q] = own_ref[:send_rows, low_end : low_end + peer_width]
    start_slab(slab_send, slab_recv, slab_sems)

    def peer_copy(o):
        to = lax.rem(t + o, peers)
        return pltpu.make_async_remote_copy(
            src_ref=peer_send.at[to],
            dst_ref=peer_recv.at[t],
            send_sem=peer_sems.at[0, o],
            recv_sem=peer_sems.at[1, t],
            device_id=(s, to),
            device_id_type=MESH,
        )

    for o in range(1, peers):
        peer_copy(o).start()
    peer_recv[t] = jnp.zeros(peer_recv.shape[1:], F32)
    theirs_ref[...] = jnp.zeros_like(theirs_ref)
    for o in range(1, peers):
        peer_copy(o).wait_send()
        origin = lax.rem(t + peers - o, peers)
        pltpu.make_async_remote_copy(
            src_ref=peer_send.at[origin],
            dst_ref=peer_recv.at[origin],
            send_sem=peer_sems.at[0, o],
            recv_sem=peer_sems.at[1, origin],
            device_id=(s, origin),
            device_id_type=MESH,
        ).wait_recv()
    for q in range(peers):
        low_end = 2 * slab_width + q * peer_width
        theirs_ref[:send_rows, low_end : low_end + peer_width] = peer_recv[q]
    finish_slab(slab_send, slab_recv, slab_sems)
    for side in range(2):
        theirs_ref[:send_rows, side * slab_width : (side + 1) * slab_width] = slab_recv[side]


def back_kernel(
    sizes,
    table_ref,
    motion_ref,
    own_ref,
    theirs_ref,
    inside_ref,
    trace_ref,
    flux_ref,
    lifting_ref,
    bound_index_ref,
    bound_values_ref,
    inner_elem_ref,
    inner_face_ref,
    inner_normal_ref,
    step_ref,
    rate_ref,
    step_out_ref,
    table,
    ones_0,
    ones_1,
    pair,
    ones_bound,
    pair_bound,
    total,
):
    num_vars, basis, rows, trace_rows, num_faces, flat_trace, chunk, tile, part = sizes
    elems = table_ref.shape[1]
    lift_rows = lifting_ref.shape[0]
    tiles, pieces = inner_elem_ref.shape[1] // tile, tile // part
    step_out_ref[0, 0] = step_ref[0, 0]
    high, low = split(table_ref[...])
    table[:rows, :] = high
    table[rows:, :] = low

    def normal_flux(jump, normal):
        product = dot(flux_ref[...], operand(jump))
        result = normal[0:1] * product[:trace_rows]
        for d in range(1, 3):
            result = result + normal[d : d + 1] * product[d * trace_rows : (d + 1) * trace_rows]
        return result

    def lifted(flux, faces):
        high = flux.astype(BF16).astype(F32)
        low = flux - high
        highs = [jnp.where(faces == k, high, 0.0).astype(BF16) for k in range(num_faces)]
        lows = [jnp.where(faces == k, low, 0.0).astype(BF16) for k in range(num_faces)]
        value = dot(lifting_ref[...], jnp.concatenate(highs + lows + highs, axis=0))
        return jnp.concatenate(split(jnp.transpose(value)), axis=1)

    def inner_index(tile_at, line):
        def of(column, wide):
            at = tile_at + column // 2
            sides = [inner_elem_ref[side : side + 1, pl.ds(at, part)] for side in range(2)]
            return jnp.concatenate(sides, axis=1)

        return of

    def chain(ones, tile_at, c):
        at = pl.multiple_of(tile_at + c * part, part)
        sides = [inner_face_ref[side : side + 1, pl.ds(at, part)] for side in range(2)]
        face = jnp.concatenate(sides, axis=1)
        columns = pl.ds(pl.multiple_of(2 * part * c, 2 * part), 2 * part)
        trace = gather_trace(
            table[...], ones[:, columns], face, trace_ref[...], rows, trace_rows, num_faces
        )
        jump = trace[:, part:] - trace[:, :part]
        bound = jnp.maximum(
            trace[flat_trace : flat_trace + 1, :part], trace[flat_trace : flat_trace + 1, part:]
        )
        flow = normal_flux(jump, inner_normal_ref[:, pl.ds(at, part)])
        drop = bound * jump
        flux = 0.5 * jnp.concatenate([flow - drop, flow + drop], axis=1)
        pair[columns, :] = lifted(flux, face)

    deep = min(256, elems)
    in_steps(
        elems,
        64,
        lambda line: fill_ones(
            ones_bound,
            line,
            64,
            lambda at, wide: bound_index_ref[0:1, at : at + wide],
            ones_bound.shape[1],
        ),
    )
    for column in range(0, ones_bound.shape[1], 2 * part):
        columns = slice(column, column + 2 * part)
        own, theirs = own_ref[:, columns], theirs_ref[:, columns]
        jump = theirs - own
        bound = jnp.maximum(
            own[flat_trace : flat_trace + 1, :], theirs[flat_trace : flat_trace + 1, :]
        )
        flux = normal_flux(jump, bound_values_ref[:, columns]) - bound * jump
        pair_bound[columns, :] = lifted(
            (0.5 * bound_values_ref[3:4, columns]) * flux, bound_index_ref[1:2, columns]
        )

    def first_scatter(line):
        lines = pl.ds(line, deep)
        total[lines, :] = dot(ones_bound[lines, :], pair_bound[...])
        fill_ones(ones_0, line, deep, inner_index(0, line), 2 * tile)

    in_steps(elems, deep, first_scatter)

    def one_tile(now, later, j):
        tile_at = pl.multiple_of(j * tile, tile)
        next_at = pl.multiple_of(jnp.minimum(j + 1, tiles - 1) * tile, tile)

        def two_chains(c, carry):
            chain(now, tile_at, 2 * c)
            chain(now, tile_at, 2 * c + 1)
            return carry

        lax.fori_loop(0, pieces // 2, two_chains, 0)

        def scatter(line):
            lines = pl.ds(line, deep)
            total[lines, :] += dot(now[lines, :], pair[...])
            fill_ones(later, line, deep, inner_index(next_at, line), 2 * tile)

        in_steps(elems, deep, scatter)

    def two_tiles(i, carry):
        one_tile(ones_0, ones_1, 2 * i)
        one_tile(ones_1, ones_0, 2 * i + 1)
        return carry

    lax.fori_loop(0, tiles // 2, two_tiles, 0)

    def finish(line):
        lines = pl.ds(line, deep)
        face_term = jnp.transpose(total[lines, :lift_rows] + total[lines, lift_rows:])
        rate = -(inside_ref[:, lines] + face_term[:rows] * motion_ref[3:4, lines])
        for b in range(basis):
            rate_ref[b, :, lines] = rate[b * num_vars : (b + 1) * num_vars]

    in_steps(elems, deep, finish)


def body(
    conserved,
    cell_size,
    sound_speed,
    jacobian,
    derivative,
    restriction,
    lifting,
    vertex_velocity,
    share_index,
    elem_vertex,
    inner_elem,
    inner_face,
    inner_normal,
    slab_elem,
    slab_face,
    slab_normal,
    peer_elem,
    peer_face,
    peer_normal,
    peer_count,
):
    num_vars, basis, elems = conserved.shape
    num_faces, face_basis = restriction.shape[:2]
    slabs, peers = lax.axis_size("shock"), lax.axis_size("trans")
    slab_width, peer_width = slab_elem.shape[1], peer_elem.shape[1]
    verts, shared = vertex_velocity.shape[1], share_index.shape[1]
    rows = up_to(num_vars * basis + 1, 16)
    lift_rows = up_to(rows, 128)
    flat_trace = num_vars * face_basis
    trace_rows = up_to(flat_trace + 1, 16)
    send_rows = up_to(flat_trace + 1, 8)
    sides = 2 * slab_width + peers * peer_width
    chunk = min(512, elems)
    part = min(128, inner_elem.shape[1])
    tile = min(4 * part, inner_elem.shape[1])

    spreads = [
        jnp.asarray(a)
        for a in selections(num_vars, basis, face_basis, num_faces, rows, lift_rows, trace_rows)
    ]
    vmem = pl.BlockSpec(memory_space=pltpu.VMEM)
    out_shapes = (
        jax.ShapeDtypeStruct((rows, elems), F32),
        jax.ShapeDtypeStruct((8, elems), F32),
        jax.ShapeDtypeStruct((8, 128), F32),
        jax.ShapeDtypeStruct((trace_rows, sides), F32),
        jax.ShapeDtypeStruct((trace_rows, sides), F32),
        jax.ShapeDtypeStruct((rows, elems), F32),
        jax.ShapeDtypeStruct((num_faces * trace_rows, 3 * rows), BF16),
        jax.ShapeDtypeStruct((3 * trace_rows, 3 * trace_rows), BF16),
        jax.ShapeDtypeStruct((lift_rows, 3 * num_faces * trace_rows), BF16),
        jax.ShapeDtypeStruct((2, sides), jnp.int32),
        jax.ShapeDtypeStruct((4, sides), F32),
    )
    front_args = [
        jnp.transpose(conserved, (1, 0, 2)),
        cell_size.reshape(1, elems),
        sound_speed.reshape(1, elems),
        vertex_velocity,
        share_index,
        elem_vertex,
        jnp.transpose(jacobian, (1, 0, 2)),
        jnp.transpose(derivative, (1, 0, 2)),
        jnp.transpose(restriction, (1, 0, 2)),
        jnp.transpose(lifting, (2, 0, 1)),
        slab_elem,
        slab_face,
        peer_elem,
        peer_face,
        slab_normal,
        peer_normal,
        jnp.transpose(peer_count),
        *spreads,
    ]
    dma = pltpu.SemaphoreType.DMA
    table, motion, step, own, theirs, inside, trace, flux, lift, bound_index, bound_values = pl.pallas_call(
        functools.partial(
            front_kernel,
            (num_vars, basis, rows, trace_rows, num_faces, slabs, peers, chunk),
        ),
        out_shape=out_shapes,
        in_specs=[vmem] * len(front_args),
        out_specs=[vmem] * len(out_shapes),
        scratch_shapes=[
            pltpu.VMEM((rows, elems), F32),
            pltpu.VMEM((rows, elems), F32),
            pltpu.VMEM((rows, elems), F32),
            pltpu.VMEM((rows, elems), F32),
            pltpu.VMEM((4 * rows, 3 * rows), BF16),
            pltpu.VMEM((elems, sides), BF16),
            pltpu.VMEM((verts + 2 * shared, elems), BF16),
            pltpu.VMEM((24, verts + 2 * shared), F32),
            pltpu.VMEM((3 * num_vars, num_vars), F32),
            pltpu.VMEM((3 * basis, basis), F32),
            pltpu.VMEM((num_faces * face_basis, basis), F32),
            pltpu.VMEM((num_faces * face_basis, basis), F32),
            pltpu.VMEM((2, 8, shared), F32),
            pltpu.VMEM((2, 8, shared), F32),
            pltpu.VMEM((peers, 8, 128), F32),
            pltpu.VMEM((slabs, 8, 128), F32),
            pltpu.VMEM((2, send_rows, slab_width), F32),
            pltpu.VMEM((2, send_rows, slab_width), F32),
            pltpu.VMEM((peers, send_rows, peer_width), F32),
            pltpu.VMEM((peers, send_rows, peer_width), F32),
            dma((4,)),
            dma((2, peers)),
            dma((2, slabs)),
            dma((4,)),
            dma((2, peers)),
        ],
        compiler_params=pltpu.CompilerParams(
            collective_id=0, has_side_effects=True, vmem_limit_bytes=VMEM_BYTES
        ),
        name="front",
    )(*front_args)

    back_args = [
        table,
        motion,
        own,
        theirs,
        inside,
        trace,
        flux,
        lift,
        bound_index,
        bound_values,
        inner_elem,
        inner_face,
        inner_normal,
        step,
    ]
    rate, step = pl.pallas_call(
        functools.partial(
            back_kernel,
            (num_vars, basis, rows, trace_rows, num_faces, flat_trace, chunk, tile, part),
        ),
        out_shape=(
            jax.ShapeDtypeStruct((basis, num_vars, elems), F32),
            jax.ShapeDtypeStruct((1, 1), F32),
        ),
        in_specs=[vmem] * (len(back_args) - 1) + [pl.BlockSpec(memory_space=pltpu.SMEM)],
        out_specs=(vmem, pl.BlockSpec(memory_space=pltpu.SMEM)),
        scratch_shapes=[
            pltpu.VMEM((2 * rows, elems), BF16),
            pltpu.VMEM((elems, 2 * tile), BF16),
            pltpu.VMEM((elems, 2 * tile), BF16),
            pltpu.VMEM((2 * tile, 2 * lift_rows), BF16),
            pltpu.VMEM((elems, sides), BF16),
            pltpu.VMEM((sides, 2 * lift_rows), BF16),
            pltpu.VMEM((elems, 2 * lift_rows), F32),
        ],
        compiler_params=pltpu.CompilerParams(vmem_limit_bytes=VMEM_BYTES),
        name="back",
    )(*back_args)
    return jnp.transpose(rate, (1, 0, 2)), step.reshape(())


def solution(mesh):
    both = ("shock", "trans")
    last2, last3 = P(None, both), P(None, None, both)
    return jax.shard_map(
        body,
        mesh=mesh,
        in_specs=(
            last3,
            P(both),
            P(both),
            P(),
            P(),
            P(),
            P(),
            last2,
            last2,
            last2,
            last2,
            last2,
            last2,
            last2,
            last2,
            last3,
            last2,
            last2,
            last3,
            last2,
        ),
        out_specs=(last3, P()),
        check_vma=False,
    )
```

```python
import functools

import jax
import jax.numpy as jnp
import numpy as np
from jax import lax
from jax.experimental import pallas as pl
from jax.experimental.pallas import tpu as pltpu
from jax.sharding import PartitionSpec as P

CFL_NUMBER = 0.3
F32 = jnp.float32
BF16 = jnp.bfloat16
MESH = pl.DeviceIdType.MESH
VMEM_BYTES = 56 * 1024 * 1024


def up_to(value, multiple):
    return -(-value // multiple) * multiple


def selections(num_vars, basis, face_basis, faces, rows, lift_rows, trace_rows):
    flat, flat_t = num_vars * basis, num_vars * face_basis
    row, trow = np.arange(rows), np.arange(trace_rows)
    row_v, row_b = (
        np.where(row < flat, row % num_vars, -1),
        np.where(row < flat, row // num_vars, -1),
    )
    lift_v, lift_b = (
        np.pad(a, (0, lift_rows - rows), constant_values=-1) for a in (row_v, row_b)
    )
    trow_v = np.where(trow < flat_t, trow // face_basis, -2)
    trow_f = np.where(trow < flat_t, trow % face_basis, -2)

    def pick(target, count):
        return (target[:, None] == np.arange(count)[None, :]).astype(np.float32)

    def block(target, count, copies):
        out = np.zeros((copies, target.size, copies * count), np.float32)
        for k in range(copies):
            out[k, :, k::copies] = pick(target, count)
        return out.reshape(copies * target.size, copies * count)

    same_v = (row_v[:, None] == row_v[None, :]) & (row_v[:, None] >= 0)
    same_vt = (lift_v[:, None] == trow_v[None, :]) & (lift_v[:, None] >= 0)
    same_tv = (trow_v[:, None] == row_v[None, :]) & (trow_v[:, None] >= 0)
    same_f = (trow_f[:, None] == trow_f[None, :]) & (trow_f[:, None] >= 0)
    keep = np.zeros((trace_rows, rows), np.float32)
    keep[flat_t, flat] = 1.0
    return [
        np.ascontiguousarray(pick(row_v, num_vars).T),
        np.ascontiguousarray(pick(row_b, basis).T),
        block(row_v, num_vars, 3),
        block(row_b, basis, 3),
        block(trow_f, face_basis, faces),
        np.ascontiguousarray(pick(trow_v, num_vars).T),
        block(trow_v, num_vars, 3),
        pick(lift_b, basis),
        np.ascontiguousarray(block(trow_f, face_basis, faces).T),
        same_v.astype(np.float32),
        same_tv.astype(np.float32),
        same_f.astype(np.float32),
        same_vt.astype(np.float32),
        keep,
    ]


def exact(a, b):
    return jnp.dot(a, b, precision=lax.Precision.HIGHEST, preferred_element_type=F32)


def dot(a, b):
    return jnp.dot(a, b, preferred_element_type=F32)


def split(value):
    high = value.astype(BF16)
    return high, (value - high.astype(F32)).astype(BF16)


def operator(matrix):
    high, low = split(matrix)
    return jnp.concatenate([high, high, low], axis=1)


def operand(value):
    high, low = split(value)
    return jnp.concatenate([high, low, high], axis=0)


def ones_at(index, count):
    places = lax.broadcasted_iota(jnp.int16, (count, index.shape[1]), 0)
    return jnp.where(places == index.astype(jnp.int16), BF16(1), BF16(0))


def apply_space(space, value, mesh_vel, inverse, rows):
    product = dot(space, operand(value))
    total = product[:rows]
    for d in range(3):
        total = total - mesh_vel[d : d + 1] * product[(d + 1) * rows : (d + 2) * rows]
    return total * inverse


def gather_trace(table, ones, faces, trace_op, rows, trace_rows, num_faces):
    found = dot(table, ones)
    high, low = found[:rows].astype(BF16), found[rows:].astype(BF16)
    every = dot(trace_op, jnp.concatenate([high, low, high], axis=0))
    trace = jnp.where(faces == 0, every[:trace_rows], 0.0)
    for k in range(1, num_faces):
        trace = trace + jnp.where(faces == k, every[k * trace_rows : (k + 1) * trace_rows], 0.0)
    return trace


def front_kernel(
    sizes,
    conserved_ref,
    size_ref,
    sound_ref,
    vertex_ref,
    share_ref,
    corner_ref,
    jac_ref,
    der_ref,
    res_ref,
    lift_ref,
    slab_elem_ref,
    slab_face_ref,
    peer_elem_ref,
    peer_face_ref,
    slab_normal_ref,
    peer_normal_ref,
    count_ref,
    sel_vt,
    sel_bt,
    sel_jac,
    sel_der,
    sel_res,
    sel_tvt,
    sel_tjac,
    sel_b,
    sel_lift,
    same_v,
    same_tv,
    same_f,
    same_vt,
    keep,
    table_ref,
    motion_ref,
    step_ref,
    own_ref,
    theirs_ref,
    space_ref,
    trace_ref,
    flux_ref,
    lifting_ref,
    bound_index_ref,
    bound_values_ref,
    state,
    first,
    second,
    ones,
    parts,
    jac,
    der,
    res,
    lift,
    vert_send,
    vert_recv,
    min_t,
    min_s,
    slab_send,
    slab_recv,
    peer_send,
    peer_recv,
    vert_sems,
    min_t_sems,
    min_s_sems,
    slab_sems,
    peer_sems,
):
    num_vars, basis, rows, trace_rows, num_faces, slabs, peers, chunk = sizes
    elems = conserved_ref.shape[2]
    shared = share_ref.shape[1]
    verts = vertex_ref.shape[1]
    slab_width = slab_send.shape[2]
    peer_width = peer_send.shape[2]
    send_rows = slab_send.shape[1]
    s = lax.axis_index("shock")
    t = lax.axis_index("trans")

    barrier = pltpu.get_barrier_semaphore()
    for o in range(1, peers):
        pl.semaphore_signal(
            barrier, inc=1, device_id=(s, lax.rem(t + o, peers)), device_id_type=MESH
        )
    for o in range(1, slabs):
        pl.semaphore_signal(
            barrier, inc=1, device_id=(lax.rem(s + o, slabs), t), device_id_type=MESH
        )

    def spread(velocity):
        high, low = split(velocity)
        rest = velocity - high.astype(F32) - low.astype(F32)
        return high.astype(F32), low.astype(F32), rest

    parts[...] = jnp.zeros_like(parts)
    for i, piece in enumerate(spread(vertex_ref[...])):
        parts[8 * i : 8 * i + 3, :verts] = piece
    share = jnp.concatenate([share_ref[0:1, :], share_ref[1:2, :]], axis=1)
    sent = dot(parts[:, :verts].astype(BF16), ones_at(share, verts))
    sent = sent[0:8] + sent[8:16] + sent[16:24]
    vert_send[0] = sent[:, :shared]
    vert_send[1] = sent[:, shared:]
    pl.semaphore_wait(barrier, peers - 1 + slabs - 1)

    def to_lower(source, dest, sems):
        return pltpu.make_async_remote_copy(
            src_ref=source.at[0],
            dst_ref=dest.at[1],
            send_sem=sems.at[0],
            recv_sem=sems.at[3],
            device_id=(s - 1, t),
            device_id_type=MESH,
        )

    def to_upper(source, dest, sems):
        return pltpu.make_async_remote_copy(
            src_ref=source.at[1],
            dst_ref=dest.at[0],
            send_sem=sems.at[1],
            recv_sem=sems.at[2],
            device_id=(s + 1, t),
            device_id_type=MESH,
        )

    def start_slab(source, dest, sems):
        @pl.when(s > 0)
        def _():
            to_lower(source, dest, sems).start()

        @pl.when(s < slabs - 1)
        def _():
            to_upper(source, dest, sems).start()

    def finish_slab(source, dest, sems):
        @pl.when(s > 0)
        def _():
            to_lower(source, dest, sems).wait_send()
            to_upper(source, dest, sems).wait_recv()

        @pl.when(s < slabs - 1)
        def _():
            to_upper(source, dest, sems).wait_send()
            to_lower(source, dest, sems).wait_recv()

        @pl.when(s == 0)
        def _():
            dest[0] = jnp.zeros(dest.shape[1:], F32)

        @pl.when(s == slabs - 1)
        def _():
            dest[1] = jnp.zeros(dest.shape[1:], F32)

    start_slab(vert_send, vert_recv, vert_sems)

    for small, held in ((jac_ref, jac), (der_ref, der), (res_ref, res), (lift_ref, lift)):
        count = small.shape[1]
        for i in range(small.shape[0]):
            held[i * count : (i + 1) * count, :] = small[i]
    jac_wide = exact(sel_jac[...], exact(jac[...], sel_vt[...]))
    der_wide = exact(sel_der[...], exact(der[...], sel_bt[...]))
    both = jac_wide * der_wide
    space_ref[0:rows, :] = operator(both[:rows] + both[rows : 2 * rows] + both[2 * rows :])
    for d in range(3):
        space_ref[(d + 1) * rows : (d + 2) * rows, :] = operator(
            der_wide[d * rows : (d + 1) * rows] * same_v[...]
        )
    for b in range(basis):
        state[b * num_vars : (b + 1) * num_vars, :] = conserved_ref[b]
    state[num_vars * basis :, :] = jnp.zeros((rows - num_vars * basis, elems), F32)

    def counted(columns, low, count):
        total = ones_at(corner_ref[0:1, columns] - low, count)
        for i in range(1, 4):
            total = total + ones_at(corner_ref[i : i + 1, columns] - low, count)
        return total

    own_parts = parts[:, :verts].astype(BF16)

    def own_corner(c, carry):
        columns = pl.ds(pl.multiple_of(c * chunk, chunk), chunk)
        found = dot(own_parts, counted(columns, 0, verts))
        motion_ref[:, columns] = found[0:8] + found[8:16] + found[16:24]
        return carry

    lax.fori_loop(0, elems // chunk, own_corner, 0)
    finish_slab(vert_send, vert_recv, vert_sems)
    for side in range(2):
        place = verts + side * shared
        for i, piece in enumerate(spread(vert_recv[side])):
            parts[8 * i : 8 * i + 8, place : place + shared] = piece
    far_parts = parts[:, verts:].astype(BF16)

    def far_corner(c, smallest):
        columns = pl.ds(pl.multiple_of(c * chunk, chunk), chunk)
        found = dot(far_parts, counted(columns, verts, 2 * shared))
        vel = 0.25 * (motion_ref[:, columns] + (found[0:8] + found[8:16] + found[16:24]))
        size = size_ref[0:1, columns]
        speed = (
            sound_ref[0:1, columns] + jnp.abs(vel[0:1]) + jnp.abs(vel[1:2]) + jnp.abs(vel[2:3])
        )
        motion_ref[0:3, columns] = vel[0:3]
        motion_ref[3:4, columns] = 1.0 / size
        motion_ref[4:5, columns] = speed
        return jnp.minimum(smallest, jnp.min(size / speed, axis=1, keepdims=True))

    smallest = lax.fori_loop(0, elems // chunk, far_corner, jnp.full((1, 1), jnp.inf, F32))

    def min_copy(buffer, sems, place, count, o, along_trans):
        to = lax.rem(place + o, count)
        return pltpu.make_async_remote_copy(
            src_ref=buffer.at[place],
            dst_ref=buffer.at[place],
            send_sem=sems.at[0, o],
            recv_sem=sems.at[1, place],
            device_id=(s, to) if along_trans else (to, t),
            device_id_type=MESH,
        )

    def min_wait(buffer, sems, place, count, along_trans):
        for o in range(1, count):
            origin = lax.rem(place + count - o, count)
            pltpu.make_async_remote_copy(
                src_ref=buffer.at[origin],
                dst_ref=buffer.at[origin],
                send_sem=sems.at[0, o],
                recv_sem=sems.at[1, origin],
                device_id=(s, origin) if along_trans else (origin, t),
                device_id_type=MESH,
            ).wait_recv()
            min_copy(buffer, sems, place, count, o, along_trans).wait_send()

    min_t[t] = jnp.broadcast_to(smallest, min_t.shape[1:])
    for o in range(1, peers):
        min_copy(min_t, min_t_sems, t, peers, o, True).start()

    def space_step(source, dest):
        def one(c, carry):
            columns = pl.ds(pl.multiple_of(c * chunk, chunk), chunk)
            dest[:, columns] = apply_space(
                space_ref[...],
                source[:, columns],
                motion_ref[:, columns],
                motion_ref[3:4, columns],
                rows,
            )
            return carry

        lax.fori_loop(0, elems // chunk, one, 0)

    space_step(state, first)
    min_wait(min_t, min_t_sems, t, peers, True)
    best = min_t[0]
    for i in range(1, peers):
        best = jnp.minimum(best, min_t[i])
    min_s[s] = best
    for o in range(1, slabs):
        min_copy(min_s, min_s_sems, s, slabs, o, False).start()
    space_step(first, second)

    res_wide = exact(sel_res[...], exact(res[...], sel_bt[...]))
    for k in range(num_faces):
        trace_ref[k * trace_rows : (k + 1) * trace_rows, :] = operator(
            res_wide[k * trace_rows : (k + 1) * trace_rows] * same_tv[...] + keep[...]
        )
    tjac_wide = exact(sel_tjac[...], exact(jac[...], sel_tvt[...]))
    for d in range(3):
        flux_ref[d * trace_rows : (d + 1) * trace_rows, :] = operator(
            tjac_wide[d * trace_rows : (d + 1) * trace_rows] * same_f[...]
        )
    lift_rows = lax.dot_general(
        sel_b[...],
        lift[...],
        (((1,), (1,)), ((), ())),
        precision=lax.Precision.HIGHEST,
        preferred_element_type=F32,
    )
    lift_wide = exact(lift_rows, sel_lift[...])
    spread_v = jnp.concatenate([same_vt[...]] * num_faces, axis=1)
    lifting_ref[...] = operator(lift_wide * spread_v)
    for row, slab_ref, peer_ref in (
        (0, slab_elem_ref, peer_elem_ref),
        (1, slab_face_ref, peer_face_ref),
    ):
        for side in range(2):
            bound_index_ref[row : row + 1, side * slab_width : (side + 1) * slab_width] = slab_ref[
                side : side + 1, :
            ]
        for q in range(peers):
            low_end = 2 * slab_width + q * peer_width
            bound_index_ref[row : row + 1, low_end : low_end + peer_width] = peer_ref[
                q : q + 1, :
            ]
    for d in range(3):
        for side in range(2):
            bound_values_ref[d : d + 1, side * slab_width : (side + 1) * slab_width] = (
                slab_normal_ref[d, side : side + 1, :]
            )
        for q in range(peers):
            low_end = 2 * slab_width + q * peer_width
            bound_values_ref[d : d + 1, low_end : low_end + peer_width] = peer_normal_ref[
                d, q : q + 1, :
            ]
    bound_values_ref[3:4, : 2 * slab_width] = jnp.ones((1, 2 * slab_width), F32)
    slot = lax.broadcasted_iota(jnp.int32, (1, peer_width), 1)
    for q in range(peers):
        low_end = 2 * slab_width + q * peer_width
        bound_values_ref[3:4, low_end : low_end + peer_width] = jnp.where(
            slot < count_ref[0:1, q : q + 1], 1.0, 0.0
        )
    ones[...] = ones_at(bound_index_ref[0:1, :], elems)

    min_wait(min_s, min_s_sems, s, slabs, False)
    best = min_s[0]
    for i in range(1, slabs):
        best = jnp.minimum(best, min_s[i])
    step = CFL_NUMBER * best
    step_ref[...] = step
    dt = step[0:1, 0:1]
    table_ref[...] = (
        state[...] - (0.5 * dt) * first[...] + (dt * dt * (1.0 / 6.0)) * second[...]
    )
    flat = num_vars * basis
    table_ref[flat : flat + 1, :] = motion_ref[4:5, :]
    high, low = split(table_ref[...])
    trace = gather_trace(
        jnp.concatenate([high, low], axis=0),
        ones[...],
        bound_index_ref[1:2, :],
        trace_ref[...],
        rows,
        trace_rows,
        num_faces,
    )
    own_ref[...] = trace
    cut = trace[:send_rows]
    slab_send[0] = cut[:, :slab_width]
    slab_send[1] = cut[:, slab_width : 2 * slab_width]
    for q in range(peers):
        low_end = 2 * slab_width + q * peer_width
        peer_send[q] = cut[:, low_end : low_end + peer_width]
    start_slab(slab_send, slab_recv, slab_sems)

    def peer_copy(o):
        to = lax.rem(t + o, peers)
        return pltpu.make_async_remote_copy(
            src_ref=peer_send.at[to],
            dst_ref=peer_recv.at[t],
            send_sem=peer_sems.at[0, o],
            recv_sem=peer_sems.at[1, t],
            device_id=(s, to),
            device_id_type=MESH,
        )

    for o in range(1, peers):
        peer_copy(o).start()
    peer_recv[t] = jnp.zeros(peer_recv.shape[1:], F32)
    theirs_ref[...] = jnp.zeros_like(theirs_ref)
    for o in range(1, peers):
        peer_copy(o).wait_send()
        origin = lax.rem(t + peers - o, peers)
        pltpu.make_async_remote_copy(
            src_ref=peer_send.at[origin],
            dst_ref=peer_recv.at[origin],
            send_sem=peer_sems.at[0, o],
            recv_sem=peer_sems.at[1, origin],
            device_id=(s, origin),
            device_id_type=MESH,
        ).wait_recv()
    for q in range(peers):
        low_end = 2 * slab_width + q * peer_width
        theirs_ref[:send_rows, low_end : low_end + peer_width] = peer_recv[q]
    finish_slab(slab_send, slab_recv, slab_sems)
    for side in range(2):
        theirs_ref[:send_rows, side * slab_width : (side + 1) * slab_width] = slab_recv[side]


def back_kernel(
    sizes,
    table_ref,
    motion_ref,
    own_ref,
    theirs_ref,
    space_ref,
    trace_ref,
    flux_ref,
    lifting_ref,
    bound_index_ref,
    bound_values_ref,
    inner_elem_ref,
    inner_face_ref,
    inner_normal_ref,
    step_ref,
    rate_ref,
    step_out_ref,
    table,
    ones,
    ones_bound,
    total,
):
    num_vars, basis, rows, trace_rows, num_faces, flat_trace, chunk, tile = sizes
    elems = table_ref.shape[1]
    lift_rows = lifting_ref.shape[0]
    step_out_ref[0, 0] = step_ref[0, 0]
    high, low = split(table_ref[...])
    table[:rows, :] = high
    table[rows:, :] = low

    def normal_flux(jump, normal):
        product = dot(flux_ref[...], operand(jump))
        result = normal[0:1] * product[:trace_rows]
        for d in range(1, 3):
            result = result + normal[d : d + 1] * product[d * trace_rows : (d + 1) * trace_rows]
        return result

    def lifted(flux, faces, where_ones):
        high = flux.astype(BF16).astype(F32)
        low = flux - high
        highs = [jnp.where(faces == k, high, 0.0).astype(BF16) for k in range(num_faces)]
        lows = [jnp.where(faces == k, low, 0.0).astype(BF16) for k in range(num_faces)]
        value = dot(lifting_ref[...], jnp.concatenate(highs + lows + highs, axis=0))
        pair = jnp.concatenate(split(value), axis=0)
        return lax.dot_general(
            where_ones, pair, (((1,), (1,)), ((), ())), preferred_element_type=F32
        )

    faces = bound_index_ref[1:2, :]
    ones_bound[...] = ones_at(bound_index_ref[0:1, :], elems)
    own, theirs = own_ref[...], theirs_ref[...]
    jump = theirs - own
    bound = jnp.maximum(
        own[flat_trace : flat_trace + 1, :], theirs[flat_trace : flat_trace + 1, :]
    )
    flux = normal_flux(jump, bound_values_ref[...]) - bound * jump
    total[...] = lifted((0.5 * bound_values_ref[3:4, :]) * flux, faces, ones_bound[...])

    def inner(j, carry):
        columns = pl.ds(pl.multiple_of(j * tile, tile), tile)
        index = jnp.concatenate(
            [inner_elem_ref[0:1, columns], inner_elem_ref[1:2, columns]], axis=1
        )
        face = jnp.concatenate(
            [inner_face_ref[0:1, columns], inner_face_ref[1:2, columns]], axis=1
        )
        ones[...] = ones_at(index, elems)
        trace = gather_trace(
            table[...], ones[...], face, trace_ref[...], rows, trace_rows, num_faces
        )
        jump = trace[:, tile:] - trace[:, :tile]
        bound = jnp.maximum(
            trace[flat_trace : flat_trace + 1, :tile], trace[flat_trace : flat_trace + 1, tile:]
        )
        flow = normal_flux(jump, inner_normal_ref[:, columns])
        drop = bound * jump
        flux = 0.5 * jnp.concatenate([flow - drop, flow + drop], axis=1)
        total[...] += lifted(flux, face, ones[...])
        return carry

    lax.fori_loop(0, inner_elem_ref.shape[1] // tile, inner, 0)

    def finish(c, carry):
        columns = pl.ds(pl.multiple_of(c * chunk, chunk), chunk)
        inverse = motion_ref[3:4, columns]
        value = apply_space(
            space_ref[...], table_ref[:, columns], motion_ref[:, columns], inverse, rows
        )
        face_term = jnp.transpose(total[columns, :lift_rows] + total[columns, lift_rows:])
        rate = -(value + face_term[:rows] * inverse)
        for b in range(basis):
            rate_ref[b, :, columns] = rate[b * num_vars : (b + 1) * num_vars]
        return carry

    lax.fori_loop(0, elems // chunk, finish, 0)


def body(
    conserved,
    cell_size,
    sound_speed,
    jacobian,
    derivative,
    restriction,
    lifting,
    vertex_velocity,
    share_index,
    elem_vertex,
    inner_elem,
    inner_face,
    inner_normal,
    slab_elem,
    slab_face,
    slab_normal,
    peer_elem,
    peer_face,
    peer_normal,
    peer_count,
):
    num_vars, basis, elems = conserved.shape
    num_faces, face_basis = restriction.shape[:2]
    slabs, peers = lax.axis_size("shock"), lax.axis_size("trans")
    slab_width, peer_width = slab_elem.shape[1], peer_elem.shape[1]
    verts, shared = vertex_velocity.shape[1], share_index.shape[1]
    rows = up_to(num_vars * basis + 1, 16)
    lift_rows = up_to(rows, 128)
    flat_trace = num_vars * face_basis
    trace_rows = up_to(flat_trace + 1, 16)
    send_rows = up_to(flat_trace + 1, 8)
    sides = 2 * slab_width + peers * peer_width
    chunk = min(512, elems)
    tile = min(512, inner_elem.shape[1])

    spreads = [
        jnp.asarray(a)
        for a in selections(num_vars, basis, face_basis, num_faces, rows, lift_rows, trace_rows)
    ]
    vmem = pl.BlockSpec(memory_space=pltpu.VMEM)
    out_shapes = (
        jax.ShapeDtypeStruct((rows, elems), F32),
        jax.ShapeDtypeStruct((8, elems), F32),
        jax.ShapeDtypeStruct((8, 128), F32),
        jax.ShapeDtypeStruct((trace_rows, sides), F32),
        jax.ShapeDtypeStruct((trace_rows, sides), F32),
        jax.ShapeDtypeStruct((4 * rows, 3 * rows), BF16),
        jax.ShapeDtypeStruct((num_faces * trace_rows, 3 * rows), BF16),
        jax.ShapeDtypeStruct((3 * trace_rows, 3 * trace_rows), BF16),
        jax.ShapeDtypeStruct((lift_rows, 3 * num_faces * trace_rows), BF16),
        jax.ShapeDtypeStruct((2, sides), jnp.int32),
        jax.ShapeDtypeStruct((4, sides), F32),
    )
    front_args = [
        jnp.transpose(conserved, (1, 0, 2)),
        cell_size.reshape(1, elems),
        sound_speed.reshape(1, elems),
        vertex_velocity,
        share_index,
        elem_vertex,
        jnp.transpose(jacobian, (1, 0, 2)),
        jnp.transpose(derivative, (1, 0, 2)),
        jnp.transpose(restriction, (1, 0, 2)),
        jnp.transpose(lifting, (2, 0, 1)),
        slab_elem,
        slab_face,
        peer_elem,
        peer_face,
        slab_normal,
        peer_normal,
        jnp.transpose(peer_count),
        *spreads,
    ]
    dma = pltpu.SemaphoreType.DMA
    table, motion, step, own, theirs, space, trace, flux, lift, bound_index, bound_values = pl.pallas_call(
        functools.partial(
            front_kernel,
            (num_vars, basis, rows, trace_rows, num_faces, slabs, peers, chunk),
        ),
        out_shape=out_shapes,
        in_specs=[vmem] * len(front_args),
        out_specs=[vmem] * len(out_shapes),
        scratch_shapes=[
            pltpu.VMEM((rows, elems), F32),
            pltpu.VMEM((rows, elems), F32),
            pltpu.VMEM((rows, elems), F32),
            pltpu.VMEM((elems, sides), BF16),
            pltpu.VMEM((24, verts + 2 * shared), F32),
            pltpu.VMEM((3 * num_vars, num_vars), F32),
            pltpu.VMEM((3 * basis, basis), F32),
            pltpu.VMEM((num_faces * face_basis, basis), F32),
            pltpu.VMEM((num_faces * face_basis, basis), F32),
            pltpu.VMEM((2, 8, shared), F32),
            pltpu.VMEM((2, 8, shared), F32),
            pltpu.VMEM((peers, 8, 128), F32),
            pltpu.VMEM((slabs, 8, 128), F32),
            pltpu.VMEM((2, send_rows, slab_width), F32),
            pltpu.VMEM((2, send_rows, slab_width), F32),
            pltpu.VMEM((peers, send_rows, peer_width), F32),
            pltpu.VMEM((peers, send_rows, peer_width), F32),
            dma((4,)),
            dma((2, peers)),
            dma((2, slabs)),
            dma((4,)),
            dma((2, peers)),
        ],
        compiler_params=pltpu.CompilerParams(
            collective_id=0, has_side_effects=True, vmem_limit_bytes=VMEM_BYTES
        ),
        name="front",
    )(*front_args)

    back_args = [
        table,
        motion,
        own,
        theirs,
        space,
        trace,
        flux,
        lift,
        bound_index,
        bound_values,
        inner_elem,
        inner_face,
        inner_normal,
        step,
    ]
    rate, step = pl.pallas_call(
        functools.partial(
            back_kernel,
            (num_vars, basis, rows, trace_rows, num_faces, flat_trace, chunk, tile),
        ),
        out_shape=(
            jax.ShapeDtypeStruct((basis, num_vars, elems), F32),
            jax.ShapeDtypeStruct((1, 1), F32),
        ),
        in_specs=[vmem] * (len(back_args) - 1) + [pl.BlockSpec(memory_space=pltpu.SMEM)],
        out_specs=(vmem, pl.BlockSpec(memory_space=pltpu.SMEM)),
        scratch_shapes=[
            pltpu.VMEM((2 * rows, elems), BF16),
            pltpu.VMEM((elems, 2 * tile), BF16),
            pltpu.VMEM((elems, sides), BF16),
            pltpu.VMEM((elems, 2 * lift_rows), F32),
        ],
        compiler_params=pltpu.CompilerParams(vmem_limit_bytes=VMEM_BYTES),
        name="back",
    )(*back_args)
    return jnp.transpose(rate, (1, 0, 2)), step.reshape(())


def solution(mesh):
    both = ("shock", "trans")
    last2, last3 = P(None, both), P(None, None, both)
    return jax.shard_map(
        body,
        mesh=mesh,
        in_specs=(
            last3,
            P(both),
            P(both),
            P(),
            P(),
            P(),
            P(),
            last2,
            last2,
            last2,
            last2,
            last2,
            last2,
            last2,
            last2,
            last3,
            last2,
            last2,
            last3,
            last2,
        ),
        out_specs=(last3, P()),
        check_vma=False,
    )
```

```python
import functools

import jax
import jax.numpy as jnp
import numpy as np
from jax import lax
from jax.experimental import pallas as pl
from jax.experimental.pallas import tpu as pltpu
from jax.sharding import PartitionSpec as P

CFL_NUMBER = 0.3
F32 = jnp.float32
BF16 = jnp.bfloat16
MESH = pl.DeviceIdType.MESH
VMEM_BYTES = 56 * 1024 * 1024


def up_to(value, multiple):
    return -(-value // multiple) * multiple


def selections(num_vars, basis, face_basis, faces, rows, lift_rows, trace_rows):
    flat, flat_t = num_vars * basis, num_vars * face_basis
    row, trow = np.arange(rows), np.arange(trace_rows)
    row_v, row_b = (
        np.where(row < flat, row % num_vars, -1),
        np.where(row < flat, row // num_vars, -1),
    )
    lift_v, lift_b = (
        np.pad(a, (0, lift_rows - rows), constant_values=-1) for a in (row_v, row_b)
    )
    trow_v = np.where(trow < flat_t, trow // face_basis, -2)
    trow_f = np.where(trow < flat_t, trow % face_basis, -2)

    def pick(target, count):
        return (target[:, None] == np.arange(count)[None, :]).astype(np.float32)

    def block(target, count, copies):
        out = np.zeros((copies, target.size, copies * count), np.float32)
        for k in range(copies):
            out[k, :, k::copies] = pick(target, count)
        return out.reshape(copies * target.size, copies * count)

    same_v = (row_v[:, None] == row_v[None, :]) & (row_v[:, None] >= 0)
    same_vt = (lift_v[:, None] == trow_v[None, :]) & (lift_v[:, None] >= 0)
    same_tv = (trow_v[:, None] == row_v[None, :]) & (trow_v[:, None] >= 0)
    same_f = (trow_f[:, None] == trow_f[None, :]) & (trow_f[:, None] >= 0)
    keep = np.zeros((trace_rows, rows), np.float32)
    keep[flat_t, flat] = 1.0
    return [
        np.ascontiguousarray(pick(row_v, num_vars).T),
        np.ascontiguousarray(pick(row_b, basis).T),
        block(row_v, num_vars, 3),
        block(row_b, basis, 3),
        block(trow_f, face_basis, faces),
        np.ascontiguousarray(pick(trow_v, num_vars).T),
        block(trow_v, num_vars, 3),
        pick(lift_b, basis),
        np.ascontiguousarray(block(trow_f, face_basis, faces).T),
        same_v.astype(np.float32),
        same_tv.astype(np.float32),
        same_f.astype(np.float32),
        same_vt.astype(np.float32),
        keep,
    ]


def exact(a, b):
    return jnp.dot(a, b, precision=lax.Precision.HIGHEST, preferred_element_type=F32)


def dot(a, b):
    return jnp.dot(a, b, preferred_element_type=F32)


def split(value):
    high = value.astype(BF16)
    return high, (value - high.astype(F32)).astype(BF16)


def operator(matrix):
    high, low = split(matrix)
    return jnp.concatenate([high, high, low], axis=1)


def operand(value):
    high, low = split(value)
    return jnp.concatenate([high, low, high], axis=0)


def ones_at(index, count):
    places = lax.broadcasted_iota(jnp.int16, (count, index.shape[1]), 0)
    return jnp.where(places == index.astype(jnp.int16), BF16(1), BF16(0))


def apply_space(space, value, mesh_vel, inverse, rows):
    product = dot(space, operand(value))
    total = product[:rows]
    for d in range(3):
        total = total - mesh_vel[d : d + 1] * product[(d + 1) * rows : (d + 2) * rows]
    return total * inverse


def gather_trace(table, ones, faces, trace_op, rows, trace_rows, num_faces):
    found = dot(table, ones)
    high, low = found[:rows].astype(BF16), found[rows:].astype(BF16)
    every = dot(trace_op, jnp.concatenate([high, low, high], axis=0))
    trace = every[(num_faces - 1) * trace_rows :]
    for k in range(num_faces - 1):
        trace = jnp.where(faces == k, every[k * trace_rows : (k + 1) * trace_rows], trace)
    return trace


def front_kernel(
    sizes,
    conserved_ref,
    size_ref,
    sound_ref,
    vertex_ref,
    share_ref,
    corner_ref,
    jac_ref,
    der_ref,
    res_ref,
    lift_ref,
    slab_elem_ref,
    slab_face_ref,
    peer_elem_ref,
    peer_face_ref,
    slab_normal_ref,
    peer_normal_ref,
    count_ref,
    sel_vt,
    sel_bt,
    sel_jac,
    sel_der,
    sel_res,
    sel_tvt,
    sel_tjac,
    sel_b,
    sel_lift,
    same_v,
    same_tv,
    same_f,
    same_vt,
    keep,
    table_ref,
    motion_ref,
    step_ref,
    own_ref,
    theirs_ref,
    space_ref,
    trace_ref,
    flux_ref,
    lifting_ref,
    bound_index_ref,
    bound_values_ref,
    state,
    first,
    second,
    ones,
    parts,
    jac,
    der,
    res,
    lift,
    vert_send,
    vert_recv,
    min_t,
    min_s,
    slab_send,
    slab_recv,
    peer_send,
    peer_recv,
    vert_sems,
    min_t_sems,
    min_s_sems,
    slab_sems,
    peer_sems,
):
    num_vars, basis, rows, trace_rows, num_faces, slabs, peers, chunk = sizes
    elems = conserved_ref.shape[2]
    shared = share_ref.shape[1]
    verts = vertex_ref.shape[1]
    slab_width = slab_send.shape[2]
    peer_width = peer_send.shape[2]
    send_rows = slab_send.shape[1]
    s = lax.axis_index("shock")
    t = lax.axis_index("trans")

    barrier = pltpu.get_barrier_semaphore()
    for o in range(1, peers):
        pl.semaphore_signal(
            barrier, inc=1, device_id=(s, lax.rem(t + o, peers)), device_id_type=MESH
        )
    for o in range(1, slabs):
        pl.semaphore_signal(
            barrier, inc=1, device_id=(lax.rem(s + o, slabs), t), device_id_type=MESH
        )

    def spread(velocity):
        high, low = split(velocity)
        rest = velocity - high.astype(F32) - low.astype(F32)
        return high.astype(F32), low.astype(F32), rest

    parts[...] = jnp.zeros_like(parts)
    for i, piece in enumerate(spread(vertex_ref[...])):
        parts[8 * i : 8 * i + 3, :verts] = piece
    share = jnp.concatenate([share_ref[0:1, :], share_ref[1:2, :]], axis=1)
    sent = dot(parts[:, :verts].astype(BF16), ones_at(share, verts))
    sent = sent[0:8] + sent[8:16] + sent[16:24]
    vert_send[0] = sent[:, :shared]
    vert_send[1] = sent[:, shared:]
    pl.semaphore_wait(barrier, peers - 1 + slabs - 1)

    def to_lower(source, dest, sems):
        return pltpu.make_async_remote_copy(
            src_ref=source.at[0],
            dst_ref=dest.at[1],
            send_sem=sems.at[0],
            recv_sem=sems.at[3],
            device_id=(s - 1, t),
            device_id_type=MESH,
        )

    def to_upper(source, dest, sems):
        return pltpu.make_async_remote_copy(
            src_ref=source.at[1],
            dst_ref=dest.at[0],
            send_sem=sems.at[1],
            recv_sem=sems.at[2],
            device_id=(s + 1, t),
            device_id_type=MESH,
        )

    def start_slab(source, dest, sems):
        @pl.when(s > 0)
        def _():
            to_lower(source, dest, sems).start()

        @pl.when(s < slabs - 1)
        def _():
            to_upper(source, dest, sems).start()

    def finish_slab(source, dest, sems):
        @pl.when(s > 0)
        def _():
            to_lower(source, dest, sems).wait_send()
            to_upper(source, dest, sems).wait_recv()

        @pl.when(s < slabs - 1)
        def _():
            to_upper(source, dest, sems).wait_send()
            to_lower(source, dest, sems).wait_recv()

        @pl.when(s == 0)
        def _():
            dest[0] = jnp.zeros(dest.shape[1:], F32)

        @pl.when(s == slabs - 1)
        def _():
            dest[1] = jnp.zeros(dest.shape[1:], F32)

    start_slab(vert_send, vert_recv, vert_sems)

    for small, held in ((jac_ref, jac), (der_ref, der), (res_ref, res), (lift_ref, lift)):
        count = small.shape[1]
        for i in range(small.shape[0]):
            held[i * count : (i + 1) * count, :] = small[i]
    jac_wide = exact(sel_jac[...], exact(jac[...], sel_vt[...]))
    der_wide = exact(sel_der[...], exact(der[...], sel_bt[...]))
    both = jac_wide * der_wide
    space_ref[0:rows, :] = operator(both[:rows] + both[rows : 2 * rows] + both[2 * rows :])
    for d in range(3):
        space_ref[(d + 1) * rows : (d + 2) * rows, :] = operator(
            der_wide[d * rows : (d + 1) * rows] * same_v[...]
        )
    for b in range(basis):
        state[b * num_vars : (b + 1) * num_vars, :] = conserved_ref[b]
    state[num_vars * basis :, :] = jnp.zeros((rows - num_vars * basis, elems), F32)

    def counted(columns, low, count):
        total = ones_at(corner_ref[0:1, columns] - low, count)
        for i in range(1, 4):
            total = total + ones_at(corner_ref[i : i + 1, columns] - low, count)
        return total

    own_parts = parts[:, :verts].astype(BF16)

    def own_corner(c, carry):
        columns = pl.ds(pl.multiple_of(c * chunk, chunk), chunk)
        found = dot(own_parts, counted(columns, 0, verts))
        motion_ref[:, columns] = found[0:8] + found[8:16] + found[16:24]
        return carry

    lax.fori_loop(0, elems // chunk, own_corner, 0)
    finish_slab(vert_send, vert_recv, vert_sems)
    for side in range(2):
        place = verts + side * shared
        for i, piece in enumerate(spread(vert_recv[side])):
            parts[8 * i : 8 * i + 8, place : place + shared] = piece
    far_parts = parts[:, verts:].astype(BF16)

    def far_corner(c, smallest):
        columns = pl.ds(pl.multiple_of(c * chunk, chunk), chunk)
        found = dot(far_parts, counted(columns, verts, 2 * shared))
        vel = 0.25 * (motion_ref[:, columns] + (found[0:8] + found[8:16] + found[16:24]))
        size = size_ref[0:1, columns]
        speed = (
            sound_ref[0:1, columns] + jnp.abs(vel[0:1]) + jnp.abs(vel[1:2]) + jnp.abs(vel[2:3])
        )
        motion_ref[0:3, columns] = vel[0:3]
        motion_ref[3:4, columns] = 1.0 / size
        motion_ref[4:5, columns] = speed
        return jnp.minimum(smallest, jnp.min(size / speed, axis=1, keepdims=True))

    smallest = lax.fori_loop(0, elems // chunk, far_corner, jnp.full((1, 1), jnp.inf, F32))

    def min_copy(buffer, sems, place, count, o, along_trans):
        to = lax.rem(place + o, count)
        return pltpu.make_async_remote_copy(
            src_ref=buffer.at[place],
            dst_ref=buffer.at[place],
            send_sem=sems.at[0, o],
            recv_sem=sems.at[1, place],
            device_id=(s, to) if along_trans else (to, t),
            device_id_type=MESH,
        )

    def min_wait(buffer, sems, place, count, along_trans):
        for o in range(1, count):
            origin = lax.rem(place + count - o, count)
            pltpu.make_async_remote_copy(
                src_ref=buffer.at[origin],
                dst_ref=buffer.at[origin],
                send_sem=sems.at[0, o],
                recv_sem=sems.at[1, origin],
                device_id=(s, origin) if along_trans else (origin, t),
                device_id_type=MESH,
            ).wait_recv()
            min_copy(buffer, sems, place, count, o, along_trans).wait_send()

    min_t[t] = jnp.broadcast_to(smallest, min_t.shape[1:])
    for o in range(1, peers):
        min_copy(min_t, min_t_sems, t, peers, o, True).start()

    def space_step(source, dest):
        def one(c, carry):
            columns = pl.ds(pl.multiple_of(c * chunk, chunk), chunk)
            dest[:, columns] = apply_space(
                space_ref[...],
                source[:, columns],
                motion_ref[:, columns],
                motion_ref[3:4, columns],
                rows,
            )
            return carry

        lax.fori_loop(0, elems // chunk, one, 0)

    space_step(state, first)
    min_wait(min_t, min_t_sems, t, peers, True)
    best = min_t[0]
    for i in range(1, peers):
        best = jnp.minimum(best, min_t[i])
    min_s[s] = best
    for o in range(1, slabs):
        min_copy(min_s, min_s_sems, s, slabs, o, False).start()
    space_step(first, second)

    res_wide = exact(sel_res[...], exact(res[...], sel_bt[...]))
    for k in range(num_faces):
        trace_ref[k * trace_rows : (k + 1) * trace_rows, :] = operator(
            res_wide[k * trace_rows : (k + 1) * trace_rows] * same_tv[...] + keep[...]
        )
    tjac_wide = exact(sel_tjac[...], exact(jac[...], sel_tvt[...]))
    for d in range(3):
        flux_ref[d * trace_rows : (d + 1) * trace_rows, :] = operator(
            tjac_wide[d * trace_rows : (d + 1) * trace_rows] * same_f[...]
        )
    lift_rows = lax.dot_general(
        sel_b[...],
        lift[...],
        (((1,), (1,)), ((), ())),
        precision=lax.Precision.HIGHEST,
        preferred_element_type=F32,
    )
    lift_wide = exact(lift_rows, sel_lift[...])
    spread_v = jnp.concatenate([same_vt[...]] * num_faces, axis=1)
    lifting_ref[...] = operator(lift_wide * spread_v)
    for row, slab_ref, peer_ref in (
        (0, slab_elem_ref, peer_elem_ref),
        (1, slab_face_ref, peer_face_ref),
    ):
        for side in range(2):
            bound_index_ref[row : row + 1, side * slab_width : (side + 1) * slab_width] = slab_ref[
                side : side + 1, :
            ]
        for q in range(peers):
            low_end = 2 * slab_width + q * peer_width
            bound_index_ref[row : row + 1, low_end : low_end + peer_width] = peer_ref[
                q : q + 1, :
            ]
    for d in range(3):
        for side in range(2):
            bound_values_ref[d : d + 1, side * slab_width : (side + 1) * slab_width] = (
                slab_normal_ref[d, side : side + 1, :]
            )
        for q in range(peers):
            low_end = 2 * slab_width + q * peer_width
            bound_values_ref[d : d + 1, low_end : low_end + peer_width] = peer_normal_ref[
                d, q : q + 1, :
            ]
    bound_values_ref[3:4, : 2 * slab_width] = jnp.ones((1, 2 * slab_width), F32)
    slot = lax.broadcasted_iota(jnp.int32, (1, peer_width), 1)
    for q in range(peers):
        low_end = 2 * slab_width + q * peer_width
        bound_values_ref[3:4, low_end : low_end + peer_width] = jnp.where(
            slot < count_ref[0:1, q : q + 1], 1.0, 0.0
        )
    ones[...] = ones_at(bound_index_ref[0:1, :], elems)

    min_wait(min_s, min_s_sems, s, slabs, False)
    best = min_s[0]
    for i in range(1, slabs):
        best = jnp.minimum(best, min_s[i])
    step = CFL_NUMBER * best
    step_ref[...] = step
    dt = step[0:1, 0:1]
    table_ref[...] = (
        state[...] - (0.5 * dt) * first[...] + (dt * dt * (1.0 / 6.0)) * second[...]
    )
    flat = num_vars * basis
    table_ref[flat : flat + 1, :] = motion_ref[4:5, :]
    high, low = split(table_ref[...])
    trace = gather_trace(
        jnp.concatenate([high, low], axis=0),
        ones[...],
        bound_index_ref[1:2, :],
        trace_ref[...],
        rows,
        trace_rows,
        num_faces,
    )
    own_ref[...] = trace
    cut = trace[:send_rows]
    slab_send[0] = cut[:, :slab_width]
    slab_send[1] = cut[:, slab_width : 2 * slab_width]
    for q in range(peers):
        low_end = 2 * slab_width + q * peer_width
        peer_send[q] = cut[:, low_end : low_end + peer_width]
    start_slab(slab_send, slab_recv, slab_sems)

    def peer_copy(o):
        to = lax.rem(t + o, peers)
        return pltpu.make_async_remote_copy(
            src_ref=peer_send.at[to],
            dst_ref=peer_recv.at[t],
            send_sem=peer_sems.at[0, o],
            recv_sem=peer_sems.at[1, t],
            device_id=(s, to),
            device_id_type=MESH,
        )

    for o in range(1, peers):
        peer_copy(o).start()
    peer_recv[t] = jnp.zeros(peer_recv.shape[1:], F32)
    theirs_ref[...] = jnp.zeros_like(theirs_ref)
    for o in range(1, peers):
        peer_copy(o).wait_send()
        origin = lax.rem(t + peers - o, peers)
        pltpu.make_async_remote_copy(
            src_ref=peer_send.at[origin],
            dst_ref=peer_recv.at[origin],
            send_sem=peer_sems.at[0, o],
            recv_sem=peer_sems.at[1, origin],
            device_id=(s, origin),
            device_id_type=MESH,
        ).wait_recv()
    for q in range(peers):
        low_end = 2 * slab_width + q * peer_width
        theirs_ref[:send_rows, low_end : low_end + peer_width] = peer_recv[q]
    finish_slab(slab_send, slab_recv, slab_sems)
    for side in range(2):
        theirs_ref[:send_rows, side * slab_width : (side + 1) * slab_width] = slab_recv[side]


def back_kernel(
    sizes,
    table_ref,
    motion_ref,
    own_ref,
    theirs_ref,
    space_ref,
    trace_ref,
    flux_ref,
    lifting_ref,
    bound_index_ref,
    bound_values_ref,
    inner_elem_ref,
    inner_face_ref,
    inner_normal_ref,
    step_ref,
    rate_ref,
    step_out_ref,
    table,
    ones,
    ones_bound,
    total,
):
    num_vars, basis, rows, trace_rows, num_faces, flat_trace, chunk, tile = sizes
    elems = table_ref.shape[1]
    lift_rows = lifting_ref.shape[0]
    step_out_ref[0, 0] = step_ref[0, 0]
    high, low = split(table_ref[...])
    table[:rows, :] = high
    table[rows:, :] = low

    def normal_flux(jump, normal):
        product = dot(flux_ref[...], operand(jump))
        result = normal[0:1] * product[:trace_rows]
        for d in range(1, 3):
            result = result + normal[d : d + 1] * product[d * trace_rows : (d + 1) * trace_rows]
        return result

    def lifted(flux, faces, where_ones):
        high, low = split(flux)
        chosen = jnp.broadcast_to(faces.astype(jnp.int16), flux.shape)
        highs = [jnp.where(chosen == k, high, BF16(0)) for k in range(num_faces)]
        lows = [jnp.where(chosen == k, low, BF16(0)) for k in range(num_faces)]
        value = dot(lifting_ref[...], jnp.concatenate(highs + lows + highs, axis=0))
        pair = jnp.concatenate(split(value), axis=0)
        found = lax.dot_general(
            where_ones, pair, (((1,), (1,)), ((), ())), preferred_element_type=F32
        )
        return found[:, :lift_rows] + found[:, lift_rows:]

    faces = bound_index_ref[1:2, :]
    ones_bound[...] = ones_at(bound_index_ref[0:1, :], elems)
    own, theirs = own_ref[...], theirs_ref[...]
    jump = theirs - own
    bound = jnp.maximum(
        own[flat_trace : flat_trace + 1, :], theirs[flat_trace : flat_trace + 1, :]
    )
    flux = normal_flux(jump, bound_values_ref[...]) - bound * jump
    total[...] = lifted((0.5 * bound_values_ref[3:4, :]) * flux, faces, ones_bound[...])

    def inner(j, carry):
        columns = pl.ds(pl.multiple_of(j * tile, tile), tile)
        index = jnp.concatenate(
            [inner_elem_ref[0:1, columns], inner_elem_ref[1:2, columns]], axis=1
        )
        face = jnp.concatenate(
            [inner_face_ref[0:1, columns], inner_face_ref[1:2, columns]], axis=1
        )
        ones[...] = ones_at(index, elems)
        trace = gather_trace(
            table[...], ones[...], face, trace_ref[...], rows, trace_rows, num_faces
        )
        jump = trace[:, tile:] - trace[:, :tile]
        bound = jnp.maximum(
            trace[flat_trace : flat_trace + 1, :tile], trace[flat_trace : flat_trace + 1, tile:]
        )
        flow = normal_flux(jump, inner_normal_ref[:, columns])
        drop = bound * jump
        flux = 0.5 * jnp.concatenate([flow - drop, flow + drop], axis=1)
        total[...] += lifted(flux, face, ones[...])
        return carry

    lax.fori_loop(0, inner_elem_ref.shape[1] // tile, inner, 0)

    def finish(c, carry):
        columns = pl.ds(pl.multiple_of(c * chunk, chunk), chunk)
        inverse = motion_ref[3:4, columns]
        value = apply_space(
            space_ref[...], table_ref[:, columns], motion_ref[:, columns], inverse, rows
        )
        face_term = jnp.transpose(total[columns, :])
        rate = -(value + face_term[:rows] * inverse)
        for b in range(basis):
            rate_ref[b, :, columns] = rate[b * num_vars : (b + 1) * num_vars]
        return carry

    lax.fori_loop(0, elems // chunk, finish, 0)


def body(
    conserved,
    cell_size,
    sound_speed,
    jacobian,
    derivative,
    restriction,
    lifting,
    vertex_velocity,
    share_index,
    elem_vertex,
    inner_elem,
    inner_face,
    inner_normal,
    slab_elem,
    slab_face,
    slab_normal,
    peer_elem,
    peer_face,
    peer_normal,
    peer_count,
):
    num_vars, basis, elems = conserved.shape
    num_faces, face_basis = restriction.shape[:2]
    slabs, peers = lax.axis_size("shock"), lax.axis_size("trans")
    slab_width, peer_width = slab_elem.shape[1], peer_elem.shape[1]
    verts, shared = vertex_velocity.shape[1], share_index.shape[1]
    rows = up_to(num_vars * basis + 1, 16)
    lift_rows = up_to(rows, 128)
    flat_trace = num_vars * face_basis
    trace_rows = up_to(flat_trace + 1, 16)
    send_rows = up_to(flat_trace + 1, 8)
    sides = 2 * slab_width + peers * peer_width
    chunk = min(512, elems)
    tile = min(512, inner_elem.shape[1])

    spreads = [
        jnp.asarray(a)
        for a in selections(num_vars, basis, face_basis, num_faces, rows, lift_rows, trace_rows)
    ]
    vmem = pl.BlockSpec(memory_space=pltpu.VMEM)
    out_shapes = (
        jax.ShapeDtypeStruct((rows, elems), F32),
        jax.ShapeDtypeStruct((8, elems), F32),
        jax.ShapeDtypeStruct((8, 128), F32),
        jax.ShapeDtypeStruct((trace_rows, sides), F32),
        jax.ShapeDtypeStruct((trace_rows, sides), F32),
        jax.ShapeDtypeStruct((4 * rows, 3 * rows), BF16),
        jax.ShapeDtypeStruct((num_faces * trace_rows, 3 * rows), BF16),
        jax.ShapeDtypeStruct((3 * trace_rows, 3 * trace_rows), BF16),
        jax.ShapeDtypeStruct((lift_rows, 3 * num_faces * trace_rows), BF16),
        jax.ShapeDtypeStruct((2, sides), jnp.int32),
        jax.ShapeDtypeStruct((4, sides), F32),
    )
    front_args = [
        jnp.transpose(conserved, (1, 0, 2)),
        cell_size.reshape(1, elems),
        sound_speed.reshape(1, elems),
        vertex_velocity,
        share_index,
        elem_vertex,
        jnp.transpose(jacobian, (1, 0, 2)),
        jnp.transpose(derivative, (1, 0, 2)),
        jnp.transpose(restriction, (1, 0, 2)),
        jnp.transpose(lifting, (2, 0, 1)),
        slab_elem,
        slab_face,
        peer_elem,
        peer_face,
        slab_normal,
        peer_normal,
        jnp.transpose(peer_count),
        *spreads,
    ]
    dma = pltpu.SemaphoreType.DMA
    table, motion, step, own, theirs, space, trace, flux, lift, bound_index, bound_values = pl.pallas_call(
        functools.partial(
            front_kernel,
            (num_vars, basis, rows, trace_rows, num_faces, slabs, peers, chunk),
        ),
        out_shape=out_shapes,
        in_specs=[vmem] * len(front_args),
        out_specs=[vmem] * len(out_shapes),
        scratch_shapes=[
            pltpu.VMEM((rows, elems), F32),
            pltpu.VMEM((rows, elems), F32),
            pltpu.VMEM((rows, elems), F32),
            pltpu.VMEM((elems, sides), BF16),
            pltpu.VMEM((24, verts + 2 * shared), F32),
            pltpu.VMEM((3 * num_vars, num_vars), F32),
            pltpu.VMEM((3 * basis, basis), F32),
            pltpu.VMEM((num_faces * face_basis, basis), F32),
            pltpu.VMEM((num_faces * face_basis, basis), F32),
            pltpu.VMEM((2, 8, shared), F32),
            pltpu.VMEM((2, 8, shared), F32),
            pltpu.VMEM((peers, 8, 128), F32),
            pltpu.VMEM((slabs, 8, 128), F32),
            pltpu.VMEM((2, send_rows, slab_width), F32),
            pltpu.VMEM((2, send_rows, slab_width), F32),
            pltpu.VMEM((peers, send_rows, peer_width), F32),
            pltpu.VMEM((peers, send_rows, peer_width), F32),
            dma((4,)),
            dma((2, peers)),
            dma((2, slabs)),
            dma((4,)),
            dma((2, peers)),
        ],
        compiler_params=pltpu.CompilerParams(
            collective_id=0, has_side_effects=True, vmem_limit_bytes=VMEM_BYTES
        ),
        name="front",
    )(*front_args)

    back_args = [
        table,
        motion,
        own,
        theirs,
        space,
        trace,
        flux,
        lift,
        bound_index,
        bound_values,
        inner_elem,
        inner_face,
        inner_normal,
        step,
    ]
    rate, step = pl.pallas_call(
        functools.partial(
            back_kernel,
            (num_vars, basis, rows, trace_rows, num_faces, flat_trace, chunk, tile),
        ),
        out_shape=(
            jax.ShapeDtypeStruct((basis, num_vars, elems), F32),
            jax.ShapeDtypeStruct((1, 1), F32),
        ),
        in_specs=[vmem] * (len(back_args) - 1) + [pl.BlockSpec(memory_space=pltpu.SMEM)],
        out_specs=(vmem, pl.BlockSpec(memory_space=pltpu.SMEM)),
        scratch_shapes=[
            pltpu.VMEM((2 * rows, elems), BF16),
            pltpu.VMEM((elems, 2 * tile), BF16),
            pltpu.VMEM((elems, sides), BF16),
            pltpu.VMEM((elems, lift_rows), F32),
        ],
        compiler_params=pltpu.CompilerParams(vmem_limit_bytes=VMEM_BYTES),
        name="back",
    )(*back_args)
    return jnp.transpose(rate, (1, 0, 2)), step.reshape(())


def solution(mesh):
    both = ("shock", "trans")
    last2, last3 = P(None, both), P(None, None, both)
    return jax.shard_map(
        body,
        mesh=mesh,
        in_specs=(
            last3,
            P(both),
            P(both),
            P(),
            P(),
            P(),
            P(),
            last2,
            last2,
            last2,
            last2,
            last2,
            last2,
            last2,
            last2,
            last3,
            last2,
            last2,
            last3,
            last2,
        ),
        out_specs=(last3, P()),
        check_vma=False,
    )
```
